128 devices in a mesh: row: 8 (over y, core), col: 8 (over x_lo, z), feat: 2 (over x_hi).
Axes of the slice: x: 4 (x_hi: 2, x_lo: 2; x = x_hi * 2 + x_lo), y: 4, z: 4, core: 2. Of those that a mesh axis runs over, the one named last changes fastest.
Arguments:
- grad_out: bfloat16 [65536, 512], P(('row', 'col'), 'feat'), may hold values from -6 to 6
- saved_agg: bfloat16 [65536, 1024], P(('row', 'col'), 'feat'), may hold values from -0.119628906 to 0.119628906
- tile_values: bfloat16 [8, 8, 640, 128, 128], P('row', 'col'), may hold values from -0.0390625 to 0.0390625
- tile_rows: int32 [8, 8, 640], P('row', 'col'), may hold values from 0 to 63, as said below
- tile_cols: int32 [8, 8, 640], P('row', 'col'), may hold values from 0 to 63
- tile_counts: int32 [8, 8], P('row', 'col'), may hold values from 40 to 640, as said below
- weight: bfloat16 [1024, 512], replicated, may hold values from -0.25 to 0.25
Outputs:
- grad_in: bfloat16 [65536, 1024], P(('row', 'col', 'feat'))
- grad_weight: float32 [1024, 512], P('feat')
The draws below stay inside these ranges and needn't reach their ends.
Inputs may be any that keep to these rules, and one draw needn't show every extreme that they name: `tile_counts`: some block has exactly 640 live slots and some block exactly 40. `tile_rows`: places may repeat within a block.
All inputs are finite; a program needn't handle non-finite values.
Results may differ from the reference program's by a relative error of at most 0.005.
Values may be sent and summed in bfloat16 or wider, within the bound.
A program may use at most 256 MiB of HBM per device.

```python
import jax
import jax.numpy as jnp
from jax import lax

FIN = 1024
FOUT = 512
TILE = 128
ROWS_DEV = 1024
TILE_MAX = 640
ROW_BLOCKS = 8
COL_BLOCKS = 8
ROW_TILES = 64
COL_TILES = 64
NODES = 65536


def place_extremes(key, upper):
    block_total = ROW_BLOCKS * COL_BLOCKS
    key_flat, key_pick = jax.random.split(key)
    values_flat = jax.random.randint(key_flat, (block_total, TILE_MAX), 0, upper)
    chosen = jax.random.randint(key_pick, (), 0, block_total)
    places = jnp.arange(block_total)
    values_flat = values_flat.at[:, 0].set(jnp.where(places == chosen, upper - 1, values_flat[:, 0]))
    values_flat = values_flat.at[:, 1].set(jnp.where(places == chosen, 0, values_flat[:, 1]))
    return values_flat.reshape(ROW_BLOCKS, COL_BLOCKS, TILE_MAX).astype(jnp.int32)


def draw_tile_rows(key, part):
    key = jax.random.fold_in(key, 5)
    return place_extremes(key, ROW_TILES)


def draw_tile_cols(key, part):
    key = jax.random.fold_in(key, 7)
    return place_extremes(key, COL_TILES)


def draw_tile_counts(key, part):
    key = jax.random.fold_in(key, 11)
    key_level, key_busy, key_light = jax.random.split(key, 3)
    block_total = ROW_BLOCKS * COL_BLOCKS
    levels = jax.random.randint(key_level, (block_total,), 1, 5)
    counts = TILE_MAX * levels * levels // 16
    busiest = jax.random.randint(key_busy, (), 0, block_total)
    lightest = (busiest + jax.random.randint(key_light, (), 1, block_total)) % block_total
    places = jnp.arange(block_total)
    counts = jnp.where(places == busiest, TILE_MAX, counts)
    counts = jnp.where(places == lightest, TILE_MAX // 16, counts)
    return counts.reshape(ROW_BLOCKS, COL_BLOCKS).astype(jnp.int32)


def shard_levels(key, dims, cuts, smallest, high):
    level, own = 1.0, jax.random.fold_in(key, 6)
    for position, blocks in cuts:
        steps = jnp.exp(jax.random.uniform(jax.random.fold_in(own, position), (blocks,), jnp.float32, smallest / len(cuts), high / len(cuts)))
        level = level * jnp.repeat(steps, dims[position] // blocks).reshape([-1 if axis == position else 1 for axis in range(len(dims))])
    return level


def scatter_about(own_key, dims, deviation, reach, cuts=(), held_as=jnp.bfloat16):
    values = jax.random.normal(own_key, dims, jnp.float32) * deviation
    if len(cuts) > 0:
        values = shard_levels(own_key, dims, cuts, -0.22, 0.18) * values
    return jnp.clip(values, min=-reach, max=reach).astype(held_as)


def setup_inputs(seed: int = 0) -> dict:
    seeds = jax.random.split(jax.random.key(seed), 8)
    grad_out = scatter_about(seeds[0], (NODES, FOUT), 1.0, 6.0, ((0, 64), (1, 2)))
    saved_agg = scatter_about(seeds[1], (NODES, FIN), 0.02, 0.119628906, ((0, 64), (1, 2)))
    tile_values = scatter_about(seeds[2], (ROW_BLOCKS, COL_BLOCKS, TILE_MAX, TILE, TILE), (TILE * TILE_MAX // 4) ** -0.5, 0.0390625, ((0, 8), (1, 8)))
    tile_rows = draw_tile_rows(jax.random.fold_in(seeds[7], 71), 0)
    tile_cols = draw_tile_cols(jax.random.fold_in(seeds[7], 71), 0)
    tile_counts = draw_tile_counts(jax.random.fold_in(seeds[7], 71), 0)
    weight = scatter_about(seeds[6], (FIN, FOUT), FOUT ** -0.5, 0.25)
    return dict(grad_out=grad_out, saved_agg=saved_agg, tile_values=tile_values, tile_rows=tile_rows, tile_cols=tile_cols, tile_counts=tile_counts, weight=weight)


def reference(grad_out, saved_agg, tile_values, tile_rows, tile_cols, tile_counts, weight):
    fine_tiles = ROWS_DEV // TILE
    tile_total = ROW_BLOCKS * COL_BLOCKS * fine_tiles
    panels = grad_out.astype(jnp.float32).reshape(tile_total, TILE, FOUT)
    slot_index = jnp.arange(TILE_MAX, dtype=jnp.int32)

    def add_block(totals, block):
        row_block = block // COL_BLOCKS
        col_block = block % COL_BLOCKS
        block_values = tile_values[row_block, col_block].astype(jnp.float32)
        block_rows = tile_rows[row_block, col_block]
        block_cols = tile_cols[row_block, col_block]
        live_mask = (slot_index < tile_counts[row_block, col_block]).astype(jnp.float32)
        global_rows = (row_block * ROW_TILES + block_rows).astype(jnp.int32)
        global_cols = (((block_cols // fine_tiles) * COL_BLOCKS + col_block) * fine_tiles + block_cols % fine_tiles).astype(jnp.int32)
        picked = panels[global_cols]
        products = jnp.einsum("kab,kbf->kaf", block_values, picked, precision=lax.Precision.HIGHEST)
        products = products * live_mask[:, None, None]
        return totals.at[global_rows].add(products), None

    empty_sum = jnp.zeros((tile_total, TILE, FOUT), jnp.float32)
    totals, unused = lax.scan(add_block, empty_sum, jnp.arange(ROW_BLOCKS * COL_BLOCKS, dtype=jnp.int32))
    hidden_grad = totals.reshape(NODES, FOUT).astype(jnp.bfloat16)
    grad_in = jnp.dot(hidden_grad, weight.T, preferred_element_type=jnp.float32).astype(jnp.bfloat16)
    grad_weight = jnp.dot(saved_agg.T, grad_out, preferred_element_type=jnp.float32)
    return grad_in, grad_weight
```

```python
import functools

import jax
import jax.numpy as jnp
from jax import lax
from jax.experimental import pallas as pl
from jax.experimental.pallas import tpu as pltpu
from jax.sharding import PartitionSpec as P

MESH = pl.DeviceIdType.MESH
F32 = jnp.float32
BF16 = jnp.bfloat16

TILE = 128
ROW_TILES = 64
SLOTS = 640
STEPS = 384
UNROLL = 8
CHUNK = 40

XR = 224
ZR = 288
XH, ZH = XR // 2, ZR // 2


def neighbours():
    row, col, feat = (lax.axis_index(a) for a in ("row", "col", "feat"))
    return row, col, feat, row // 2, row % 2, col // 4, col % 4


def greet(devices):
    barrier = pltpu.get_barrier_semaphore()
    for d in devices:
        pl.semaphore_signal(barrier, inc=1, device_id=d, device_id_type=MESH)
    pl.semaphore_wait(barrier, len(devices))


def gather_kernel(x_ref, saved_ref, panel, gw_ref, other, ssem, rsem, lsem):
    row, col, feat, y, core, _, _ = neighbours()
    up = (((y + 1) % 4) * 2 + core, col, feat)
    down = (((y + 3) % 4) * 2 + core, col, feat)
    twin = (y * 2 + 1 - core, col, feat)
    mate = (row, col, 1 - feat)
    half = x_ref.shape[0] // 2
    lo, hi, whole = pl.ds(0, half), pl.ds(half, half), pl.ds(0, 2 * half)
    r_up, r_down, r_far = (((y + k) % 4) * 2 + core for k in (1, 3, 2))

    def send(i, src, r, part, to):
        return pltpu.make_async_remote_copy(
            src_ref=src.at[part],
            dst_ref=panel.at[r, part],
            send_sem=ssem.at[i],
            recv_sem=rsem.at[i],
            device_id=to,
            device_id_type=MESH,
        )

    greet((up, down, twin, mate))
    c = {}
    c[0] = send(0, x_ref, row, lo, up)
    c[1] = send(1, x_ref, row, hi, down)
    c[2] = send(2, x_ref, row, hi, up)
    c[3] = send(3, x_ref, row, lo, down)
    c[4] = send(4, x_ref, row, whole, twin)
    c[11] = pltpu.make_async_remote_copy(
        src_ref=x_ref, dst_ref=other, send_sem=ssem.at[11], recv_sem=rsem.at[11],
        device_id=mate, device_id_type=MESH,
    )
    for i in (0, 1, 11, 2, 3, 4):
        c[i].start()
    own = pltpu.make_async_copy(x_ref, panel.at[row], lsem.at[0])
    own.start()

    def term(source, slot):
        def columns(n, _):
            at = pl.ds(pl.multiple_of(n * 128, 128), 128)
            gw_ref[slot, at, :] = lax.dot_general(
                saved_ref[:, at], source[...], (((0,), (0,)), ((), ())),
                preferred_element_type=F32,
            ).astype(BF16)
            return 0

        lax.fori_loop(0, saved_ref.shape[1] // 128, columns, 0)

    c[0].wait_recv()
    c[5] = send(5, panel.at[r_down], r_down, lo, up)
    c[5].start()
    c[1].wait_recv()
    c[6] = send(6, panel.at[r_up], r_up, hi, down)
    c[6].start()
    term(x_ref, feat)
    c[2].wait_recv()
    c[7] = send(7, panel.at[r_down], r_down, whole, twin)
    c[7].start()
    c[3].wait_recv()
    c[8] = send(8, panel.at[r_up], r_up, whole, twin)
    c[8].start()
    c[5].wait_recv()
    c[9] = send(9, panel.at[r_far], r_far, lo, twin)
    c[9].start()
    c[6].wait_recv()
    c[10] = send(10, panel.at[r_far], r_far, hi, twin)
    c[10].start()
    c[11].wait_recv()
    term(other, 1 - feat)
    for i in (4, 7, 8, 9, 10):
        c[i].wait_recv()
    own.wait()
    for i in range(12):
        c[i].wait_send()


def gather(x, saved):
    rows, width = x.shape
    return pl.pallas_call(
        gather_kernel,
        out_shape=(
            jax.ShapeDtypeStruct((8, rows, width), BF16),
            jax.ShapeDtypeStruct((2, saved.shape[1], width), BF16),
        ),
        in_specs=[pl.BlockSpec(memory_space=pltpu.VMEM)] * 2,
        out_specs=(pl.BlockSpec(memory_space=pl.ANY), pl.BlockSpec(memory_space=pltpu.VMEM)),
        scratch_shapes=[
            pltpu.VMEM((rows, width), BF16),
            pltpu.SemaphoreType.DMA((12,)),
            pltpu.SemaphoreType.DMA((12,)),
            pltpu.SemaphoreType.DMA((1,)),
        ],
        compiler_params=pltpu.CompilerParams(
            collective_id=0, has_side_effects=True, vmem_limit_bytes=32 * 2**20
        ),
        name="gather",
    )(x, saved)


def product_kernel(word, info, size, tiles, panel, out, held, sems):
    count, steps = size[0], size[1]

    def chunk(n):
        at = pl.ds(n * CHUNK, CHUNK)
        return pltpu.make_async_copy(tiles.at[at], held.at[at], sems.at[n])

    for n in range(SLOTS // CHUNK):
        @pl.when(n * CHUNK < count)
        def _():
            chunk(n).start()

    held[SLOTS] = jnp.zeros((TILE, TILE), BF16)
    for n in range(SLOTS // CHUNK):
        @pl.when(n * CHUNK < count)
        def _():
            chunk(n).wait()

    def group(g, total):
        for u in range(UNROLL):
            p = g * UNROLL + u
            a, b, at = word[2 * p], word[2 * p + 1], info[p]
            left = jnp.concatenate([held[a // 64], held[b // 64]], axis=1)
            right = jnp.concatenate([panel[a % 64], panel[b % 64]], axis=0)
            fresh = jnp.dot(left, right, preferred_element_type=F32)
            total = fresh + jnp.where(at % 2 == 1, 0.0, total)
            out[at // 2] = total.astype(BF16)
        return total

    lax.fori_loop(
        0, (steps + UNROLL - 1) // UNROLL, group, jnp.zeros((TILE, panel.shape[2]), F32)
    )


def tile_products(word, info, size, tiles, panel):
    width = panel.shape[2]
    return pl.pallas_call(
        product_kernel,
        grid_spec=pltpu.PrefetchScalarGridSpec(
            num_scalar_prefetch=3,
            grid=(1,),
            in_specs=[
                pl.BlockSpec(memory_space=pl.ANY),
                pl.BlockSpec((ROW_TILES, TILE, width), lambda *_: (0, 0, 0)),
            ],
            out_specs=pl.BlockSpec((ROW_TILES, TILE, width), lambda *_: (0, 0, 0)),
            scratch_shapes=[
                pltpu.VMEM((SLOTS + 1, TILE, TILE), BF16),
                pltpu.SemaphoreType.DMA((SLOTS // CHUNK,)),
            ],
        ),
        out_shape=jax.ShapeDtypeStruct((ROW_TILES, TILE, width), BF16),
        compiler_params=pltpu.CompilerParams(vmem_limit_bytes=56 * 2**20),
        name="tile_products",
    )(word, info, size, tiles, panel)


def plan(rows, cols, count):
    slot = jnp.arange(SLOTS, dtype=jnp.int32)
    row = jnp.arange(ROW_TILES, dtype=jnp.int32)
    rows = jnp.where(slot < count, rows, ROW_TILES)
    held = jnp.sum((rows[None, :] == row[:, None]).astype(jnp.int32), axis=1)
    padded = jnp.maximum(held + held % 2, 2)
    end = jnp.sum(jnp.where(row[None, :] <= row[:, None], padded[None, :], 0), axis=1)
    start = end - padded
    before = jnp.sum(
        ((rows[None, :] == rows[:, None]) & (slot[None, :] < slot[:, None])).astype(jnp.int32), axis=1
    )
    first = jnp.sum(jnp.where(rows[:, None] == row[None, :], start[None, :], 0), axis=1)
    place = jnp.where(slot < count, first + before, 4 * STEPS)
    at = jnp.arange(2 * STEPS, dtype=jnp.int32)
    empty = SLOTS * 64
    word = empty + jnp.sum(
        jnp.where(place[None, :] == at[:, None], (slot * 64 + cols - empty)[None, :], 0), axis=1
    )
    step = 2 * jnp.arange(STEPS, dtype=jnp.int32)
    row_of = jnp.minimum(
        jnp.sum((end[None, :] <= step[:, None]).astype(jnp.int32), axis=1), ROW_TILES - 1
    )
    opens = jnp.sum((start[None, :] == step[:, None]).astype(jnp.int32), axis=1)
    size = jnp.stack([count, end[ROW_TILES - 1] // 2])
    return word, row_of * 2 + opens, size


def reduce_kernel(
    part, gw, weight, grad_in, grad_weight,
    z1p, z1m, z2p, z2m, zsp, zsm, xs, xr,
    xb, x1p, x1m, x2p, x2m, xw, xsp, xsm,
    give, got, kept, total,
    ar1, ar2s, ar2, ar3, ar4,
    ssem, rsem,
):
    row, col, feat, y, core, x, z = neighbours()
    zp, zm, zf = (z + 1) % 4, (z + 3) % 4, (z + 2) % 4
    up, down = (row, x * 4 + zp, feat), (row, x * 4 + zm, feat)
    twin = (row, (1 - x) * 4 + z, feat)
    cross = (row, (1 - x) * 4 + z, 1 - feat)
    others_r = [((row + j) % 8, col, feat) for j in range(1, 8)]
    others_c = [(row, (col + j) % 8, feat) for j in range(1, 8)]
    quarter = ((1 - x, feat), (x, 1 - feat), (x, feat), (1 - x, 1 - feat))
    r_x = pl.ds(0, XR)
    r_a, r_b = pl.ds(XR, ZH), pl.ds(XR + ZH, ZH)
    v_a, v_b = pl.ds(0, ZH), pl.ds(ZH, ZH)
    w_a, w_b = pl.ds(0, XH), pl.ds(XH, XH)
    started = []

    def send(src, dst, to):
        i = len(started)
        copy = pltpu.make_async_remote_copy(
            src_ref=src, dst_ref=dst, send_sem=ssem.at[i], recv_sem=rsem.at[i],
            device_id=to, device_id_type=MESH,
        )
        copy.start()
        started.append(copy)
        return copy

    def own(q, zz, rows):
        xx, h = quarter[q]
        return part.at[xx, zz, h, rows]

    def f32(ref):
        return ref[...].astype(F32)

    greet(others_r + others_c + [cross])

    hop_p, hop_m, plain_p, plain_m, sum_p, sum_m = {}, {}, {}, {}, {}, {}
    far = (zf, zp, zm, z)
    xhop = {}
    for k in range(2):
        xhop[0, k] = send(own(k, zf, r_x), xb.at[0, k], twin)
    for q in range(4):
        hop_p[q] = send(own(q, zf, r_a), z1p.at[q], up)
        hop_m[q] = send(own(q, zf, r_b), z1m.at[q], down)
    for o in range(1, 4):
        for k in range(2):
            xhop[o, k] = send(own(k, far[o], r_x), xb.at[o, k], twin)
    for q in range(4):
        plain_p[q] = send(own(q, zp, r_b), z2p.at[q, v_b], up)
        plain_m[q] = send(own(q, zm, r_a), z2m.at[q, v_a], down)
    ar1c = [send(gw.at[:, (row + j) % 8], ar1.at[j - 1], others_r[j - 1]) for j in range(1, 8)]

    for q in range(4):
        hop_p[q].wait_recv()
        zsp[q] = (f32(z1p.at[q]) + f32(own(q, zp, r_a))).astype(BF16)
        sum_p[q] = send(zsp.at[q], z2p.at[q, v_a], up)
        hop_m[q].wait_recv()
        zsm[q] = (f32(z1m.at[q]) + f32(own(q, zm, r_b))).astype(BF16)
        sum_m[q] = send(zsm.at[q], z2m.at[q, v_b], down)

    x1c = []
    for k in range(2):
        xhop[0, k].wait_recv()
        xw[k] = (f32(xb.at[0, k]) + f32(own(2 + k, zf, r_x))).astype(BF16)
        x1c.append((send(xw.at[k, w_a], x1p.at[k], up), send(xw.at[k, w_b], x1m.at[k], down)))

    for c in ar1c:
        c.wait_recv()
    acc = gw[:, row].astype(F32)
    for j in range(7):
        acc = acc + ar1[j].astype(F32)
    for s in range(8):
        ar2s[s] = acc[:, s * 8 : s * 8 + 8, :]
    ar2c = [send(ar2s.at[(col + j) % 8], ar2.at[j - 1], others_c[j - 1]) for j in range(1, 8)]

    x2c = []
    for k in range(2):
        xhop[1, k].wait_recv()
        x1c[k][0].wait_recv()
        mine = own(2 + k, zp, r_x)
        xsp[k, w_a] = (f32(xb.at[1, k, w_a]) + f32(mine.at[w_a]) + f32(x1p.at[k])).astype(BF16)
        xsp[k, w_b] = (f32(xb.at[1, k, w_b]) + f32(mine.at[w_b])).astype(BF16)
        up_copy = send(xsp.at[k], x2p.at[k], up)
        xhop[2, k].wait_recv()
        x1c[k][1].wait_recv()
        mine = own(2 + k, zm, r_x)
        xsm[k, w_a] = (f32(xb.at[2, k, w_a]) + f32(mine.at[w_a])).astype(BF16)
        xsm[k, w_b] = (f32(xb.at[2, k, w_b]) + f32(mine.at[w_b]) + f32(x1m.at[k])).astype(BF16)
        x2c.append((up_copy, send(xsm.at[k], x2m.at[k], down)))

    for c in ar2c:
        c.wait_recv()
    done = ar2s[col]
    for j in range(7):
        done = done + ar2[j]
    ar3[col] = done
    ar3c = [send(ar3.at[col], ar3.at[col], others_c[j]) for j in range(7)]

    def zsum(q):
        for c in (plain_p[q], plain_m[q], sum_p[q], sum_m[q]):
            c.wait_recv()
        return f32(own(q, z, pl.ds(XR, ZR))) + f32(z2p.at[q]) + f32(z2m.at[q])

    xc = []
    for k in range(2):
        xs[k] = zsum(k).astype(BF16)
        xc.append(send(xs.at[k], xr.at[k], twin))

    for c in ar3c:
        c.wait_recv()
    for s in range(8):
        total[:, s * 8 : s * 8 + 8, :] = ar3[s]
    ar4[row] = total[...].astype(BF16)
    ar4c = [send(ar4.at[row], ar4.at[row], others_r[j]) for j in range(7)]

    at_z = pl.ds(XR, ZR)
    z_kept = zsum(3)
    xc[1].wait_recv()
    give[at_z] = (z_kept + f32(xr.at[1])).astype(BF16)
    give_z = send(give.at[at_z], got.at[at_z], cross)
    z_kept = zsum(2)
    xc[0].wait_recv()
    kept[at_z] = (z_kept + f32(xr.at[0])).astype(BF16)

    def xsum(k):
        xhop[3, k].wait_recv()
        for c in x2c[k]:
            c.wait_recv()
        return f32(xb.at[3, k]) + f32(own(2 + k, z, r_x)) + f32(x2p.at[k]) + f32(x2m.at[k])

    give[r_x] = xsum(1).astype(BF16)
    give_x = send(give.at[r_x], got.at[r_x], cross)
    kept[r_x] = xsum(0).astype(BF16)

    for c in ar4c:
        c.wait_recv()
    for r in range(8):
        for f in range(2):
            grad_weight[r * 64 : r * 64 + 64, f * 256 : f * 256 + 256] = ar4[r, f].astype(F32)
    give_z.wait_recv()
    give_x.wait_recv()

    w_own = pl.ds(pl.multiple_of(feat * 256, 256), 256)
    w_other = pl.ds(pl.multiple_of((1 - feat) * 256, 256), 256)

    def columns(n, _):
        at = pl.ds(pl.multiple_of(n * 256, 256), 256)
        dims = (((1,), (1,)), ((), ()))
        value = lax.dot_general(kept[...], weight[at, w_own], dims, preferred_element_type=F32)
        value += lax.dot_general(got[...], weight[at, w_other], dims, preferred_element_type=F32)
        grad_in[:, at] = value.astype(BF16)
        return 0

    lax.fori_loop(0, weight.shape[0] // 256, columns, 0)
    for c in started:
        c.wait_send()


def reduce(part, gw, weight):
    vmem = pl.BlockSpec(memory_space=pltpu.VMEM)
    scratch = [
        ((4, ZH, 256), BF16), ((4, ZH, 256), BF16),
        ((4, ZR, 256), BF16), ((4, ZR, 256), BF16),
        ((4, ZH, 256), BF16), ((4, ZH, 256), BF16),
        ((2, ZR, 256), BF16), ((2, ZR, 256), BF16),
        ((4, 2, XR, 256), BF16),
        ((2, XH, 256), BF16), ((2, XH, 256), BF16),
        ((2, XR, 256), BF16), ((2, XR, 256), BF16),
        ((2, XR, 256), BF16), ((2, XR, 256), BF16), ((2, XR, 256), BF16),
        ((512, 256), BF16), ((512, 256), BF16), ((512, 256), BF16),
        ((2, 64, 256), F32),
        ((7, 2, 64, 256), BF16), ((8, 2, 8, 256), F32), ((7, 2, 8, 256), F32),
        ((8, 2, 8, 256), F32), ((8, 2, 64, 256), BF16),
    ]
    return pl.pallas_call(
        reduce_kernel,
        out_shape=(
            jax.ShapeDtypeStruct((512, 1024), BF16),
            jax.ShapeDtypeStruct((512, 512), F32),
        ),
        in_specs=[vmem] * 3,
        out_specs=(vmem, vmem),
        scratch_shapes=[pltpu.VMEM(s, t) for s, t in scratch]
        + [pltpu.SemaphoreType.DMA((80,)), pltpu.SemaphoreType.DMA((80,))],
        compiler_params=pltpu.CompilerParams(
            collective_id=1, has_side_effects=True, vmem_limit_bytes=48 * 2**20
        ),
        name="reduce",
    )(part, gw, weight)


def per_device(grad_out, saved_agg, tile_values, tile_rows, tile_cols, tile_counts, weight):
    word, info, size = plan(tile_rows[0, 0], tile_cols[0, 0], tile_counts[0, 0])
    panel, gw = gather(grad_out, saved_agg)
    part = tile_products(
        word, info, size, tile_values[0, 0], panel.reshape(ROW_TILES, TILE, grad_out.shape[1])
    )
    return reduce(
        part.reshape(2, 4, 2, 512, 256), gw.reshape(2, 8, 64, 256), weight
    )


def solution(mesh):
    in_specs = (
        P(("row", "col"), "feat"),
        P(("row", "col"), "feat"),
        P("row", "col", None, None, None),
        P("row", "col", None),
        P("row", "col", None),
        P("row", "col"),
        P(),
    )
    out_specs = (P(("row", "col", "feat"), None), P("feat", None))
    return jax.shard_map(
        per_device, mesh=mesh, in_specs=in_specs, out_specs=out_specs, check_vma=False
    )
```

```python
import jax
import jax.numpy as jnp
from jax import lax
from jax.experimental import pallas as pl
from jax.experimental.pallas import tpu as pltpu
from jax.sharding import PartitionSpec as P

MESH = pl.DeviceIdType.MESH
F32 = jnp.float32
BF16 = jnp.bfloat16
I32 = jnp.int32

TILE = 128
ROW_TILES = 64
SLOTS = 640
FOURS = 208
PLACES = 896
UNROLL = 16
CHUNKS = 16
WIDE = 128

XR = 224
ZR = 288
XH, ZH = XR // 2, ZR // 2
GIVE, KEEP = pl.ds(0, 2), pl.ds(2, 2)


def fused_kernel(
    rows_ref, cols_ref, count_ref, x_hbm, saved_hbm, tiles_hbm, weight_hbm,
    grad_in, grad_weight,
    held, panel0, panel1, slots, part,
    z1p, z1m, z2p, z2m, zsp, zsm, xs, xr, xb, x1p, x1m, x2p, x2m, xw, xsp, xsm,
    give, got, kept, saved, weight, other, gw, total_gw,
    ar1, ar2s, ar2, ar3, ar4,
    table_v, last_v, table, last,
    ssem, rsem, lsem,
):
    row, col, feat = (lax.axis_index(a) for a in ("row", "col", "feat"))
    y, core, x, z = row // 2, row % 2, col // 4, col % 4
    panels = (panel0, panel1)
    y_up = (((y + 1) % 4) * 2 + core, col, feat)
    y_down = (((y + 3) % 4) * 2 + core, col, feat)
    chip_mate = (y * 2 + 1 - core, col, feat)
    mate = (row, col, 1 - feat)
    up, down = (row, x * 4 + (z + 1) % 4, feat), (row, x * 4 + (z + 3) % 4, feat)
    twin = (row, (1 - x) * 4 + z, feat)
    cross = (row, (1 - x) * 4 + z, 1 - feat)
    others_r = [((row + j) % 8, col, feat) for j in range(1, 8)]
    others_c = [(row, (col + j) % 8, feat) for j in range(1, 8)]
    started = []

    def send(src, dst, to):
        i = len(started)
        copy = pltpu.make_async_remote_copy(
            src_ref=src, dst_ref=dst, send_sem=ssem.at[i], recv_sem=rsem.at[i],
            device_id=to, device_id_type=MESH,
        )
        copy.start()
        started.append(copy)
        return copy

    def f32(value):
        return value.astype(F32)

    local = []
    for h in range(2):
        local.append(
            pltpu.make_async_copy(
                x_hbm.at[:, :, pl.ds(h * WIDE, WIDE)], panels[h].at[pl.ds(row * 8, 8)], lsem.at[h]
            )
        )
    local.append(pltpu.make_async_copy(saved_hbm, saved, lsem.at[2]))
    local.append(pltpu.make_async_copy(weight_hbm, weight, lsem.at[3]))
    each = SLOTS // CHUNKS
    for n in range(CHUNKS):
        at = pl.ds(n * each, each)
        local.append(pltpu.make_async_copy(tiles_hbm.at[at], held.at[at], lsem.at[4 + n]))
    for c in local:
        c.start()

    barrier = pltpu.get_barrier_semaphore()
    friends = others_r + others_c + [mate, cross]
    for d in friends:
        pl.semaphore_signal(barrier, inc=1, device_id=d, device_id_type=MESH)
    pl.semaphore_wait(barrier, len(friends))

    r_down, r_up, r_far = (((y + k) % 4) * 2 + core for k in (3, 1, 2))

    def shard(h, r, half=None):
        at = pl.ds(r * 8, 8) if half is None else pl.ds(r * 8 + half * 4, 4)
        return panels[h].at[at]

    def pass_on(h, r, to, half=None):
        return send(shard(h, r, half), shard(h, r, half), to)

    ag = ({}, {})

    def gather_first(h):
        a = ag[h]
        a["up0"], a["down1"] = pass_on(h, row, y_up, 0), pass_on(h, row, y_down, 1)
        a["up1"], a["down0"] = pass_on(h, row, y_up, 1), pass_on(h, row, y_down, 0)
        a["core"] = pass_on(h, row, chip_mate)

    def gather_far(h):
        a = ag[h]
        a["up0"].wait_recv()
        a["far0"] = pass_on(h, r_down, y_up, 0)
        a["down1"].wait_recv()
        a["far1"] = pass_on(h, r_up, y_down, 1)

    def gather_near(h):
        a = ag[h]
        a["up1"].wait_recv()
        a["core_d"] = pass_on(h, r_down, chip_mate)
        a["down0"].wait_recv()
        a["core_u"] = pass_on(h, r_up, chip_mate)

    def gather_last(h):
        a = ag[h]
        a["far0"].wait_recv()
        a["core_f0"] = pass_on(h, r_far, chip_mate, 0)
        a["far1"].wait_recv()
        a["core_f1"] = pass_on(h, r_far, chip_mate, 1)

    def gather_end(h):
        for name in ("core", "core_d", "core_u", "core_f0", "core_f1"):
            ag[h][name].wait_recv()

    local[0].wait()
    gather_first(0)
    swap = [send(x_hbm.at[:, :, pl.ds(h * WIDE, WIDE)], other.at[h], mate) for h in range(2)]

    def iota(shape, axis):
        return lax.broadcasted_iota(I32, shape, axis)

    def total(mask, value, axis):
        return jnp.sum(jnp.where(mask, value, 0), axis=axis, keepdims=True)

    count = count_ref[0, 0]
    slot_r = iota((1, SLOTS), 1)
    slot_c = iota((SLOTS, 1), 0)
    eye = iota((SLOTS, SLOTS), 0) == iota((SLOTS, SLOTS), 1)
    rows_r = jnp.where(slot_r < count, rows_ref[...], ROW_TILES)
    rows_c = total(eye, rows_r, 1)
    cols_c = total(eye, cols_ref[...], 1)
    tile_r, tile_c = iota((1, TILE), 1), iota((TILE, 1), 0)
    n_c = total(rows_r == tile_c, 1, 1)
    n_r = total(rows_c == tile_r, 1, 0)
    n_c = jnp.where(tile_c < ROW_TILES, (n_c + 3) >> 2, 0)
    n_r = jnp.where(tile_r < ROW_TILES, (n_r + 3) >> 2, 0)
    end_r = total(tile_c <= tile_r, n_c, 0)
    start_r = end_r - n_r
    before = total((rows_r == rows_c) & (slot_r < slot_c), 1, 1)
    first = total(rows_c == tile_r, start_r, 1)
    place = jnp.where(rows_c < ROW_TILES, first * 4 + before, PLACES)
    at_r = iota((1, PLACES), 1)
    empty = SLOTS * 64
    word = total(place == at_r, slot_c * 64 + cols_c - empty, 0) + empty
    start_c = total(tile_c == tile_r, start_r, 1)
    opens = total((start_c * 4 == at_r) & (n_c > 0), 1, 0)
    table_v[...] = word + opens * 65536
    last_v[...] = jnp.where(n_r > 0, end_r - 1, FOURS)
    fill = [
        pltpu.make_async_copy(table_v, table, lsem.at[20]),
        pltpu.make_async_copy(last_v, last, lsem.at[21]),
    ]
    for c in fill:
        c.start()

    gather_far(0)
    local[1].wait()
    gather_first(1)

    def term(low, high, slot):
        def columns(n, _):
            at = pl.ds(pl.multiple_of(n * 128, 128), 128)
            source = jnp.concatenate([low().reshape(8 * TILE, WIDE), high().reshape(8 * TILE, WIDE)], axis=1)
            value = lax.dot_general(
                saved[:, at], source, (((0,), (0,)), ((), ())), preferred_element_type=F32
            )
            gw[slot, pl.ds(n * 2, 2)] = value.astype(BF16).reshape(2, 64, 256)
            return 0

        lax.fori_loop(0, 4, columns, 0)

    local[2].wait()
    mine = pl.ds(row * 8, 8)
    term(lambda: panel0[mine], lambda: panel1[mine], feat)
    gather_near(0)
    held[SLOTS] = jnp.zeros((TILE, TILE), BF16)
    slots[FOURS] = jnp.zeros((TILE, WIDE), BF16)
    for c in local[3:] + fill:
        c.wait()
    gather_last(0)
    gather_end(0)

    def products(h, lo, hi, sums):
        panel = panels[h]

        def group(g, sums):
            for u in range(UNROLL):
                p = g * UNROLL + u
                w = [table[0, 4 * p + i] for i in range(4)]
                left = jnp.concatenate([held[(a >> 6) & 1023] for a in w], axis=1)
                right = jnp.concatenate([panel[a & 63] for a in w], axis=0)
                fresh = jnp.dot(left, right, preferred_element_type=F32)
                sums = fresh + jnp.where((w[0] >> 16) > 0, 0.0, sums)
                slots[p] = sums.astype(BF16)
            return sums

        return lax.fori_loop(lo, hi, group, sums)

    quarters = ((1 - x, feat), (x, 1 - feat), (x, feat), (1 - x, 1 - feat))
    offsets = (2, 1, 3, 0)

    def collect(h):
        for o in range(4):
            for q in range(4):
                xx, half = quarters[q]
                base = (xx * 4 + (z + offsets[o]) % 4) * 8 + half * 4
                for t in range(4):
                    part[h, o, q, t * TILE : (t + 1) * TILE] = slots[last[0, base + t]]

    r_x, r_z = pl.ds(0, XR), pl.ds(XR, ZR)
    r_a, r_b = pl.ds(XR, ZH), pl.ds(XR + ZH, ZH)
    v_a, v_b = pl.ds(0, ZH), pl.ds(ZH, ZH)
    w_a, w_b = pl.ds(0, XH), pl.ds(XH, XH)
    rs = ({}, {})
    pair = (GIVE, KEEP)

    def xhop(h, o):
        rs[h]["xhop", o] = send(part.at[h, o, GIVE, r_x], xb.at[h, o], twin)

    def hop(h, g):
        s, at = rs[h], pair[g]
        s["hop_p", g] = send(part.at[h, 0, at, r_a], z1p.at[h, at], up)
        s["hop_m", g] = send(part.at[h, 0, at, r_b], z1m.at[h, at], down)

    def plain(h, g):
        s, at = rs[h], pair[g]
        s["plain_p", g] = send(part.at[h, 1, at, r_b], z2p.at[h, at, v_b], up)
        s["plain_m", g] = send(part.at[h, 2, at, r_a], z2m.at[h, at, v_a], down)

    def sums(h, g):
        s, at = rs[h], pair[g]
        s["hop_p", g].wait_recv()
        zsp[h, at] = (f32(z1p[h, at]) + f32(part[h, 1, at, r_a])).astype(BF16)
        s["sum_p", g] = send(zsp.at[h, at], z2p.at[h, at, v_a], up)
        s["hop_m", g].wait_recv()
        zsm[h, at] = (f32(z1m[h, at]) + f32(part[h, 2, at, r_b])).astype(BF16)
        s["sum_m", g] = send(zsm.at[h, at], z2m.at[h, at, v_b], down)

    def x_first(h):
        s = rs[h]
        s["xhop", 0].wait_recv()
        xw[h] = (f32(xb[h, 0]) + f32(part[h, 0, KEEP, r_x])).astype(BF16)
        s["x1p"] = send(xw.at[h, :, w_a], x1p.at[h], up)
        s["x1m"] = send(xw.at[h, :, w_b], x1m.at[h], down)

    def x_second(h):
        s = rs[h]
        s["xhop", 1].wait_recv()
        s["x1p"].wait_recv()
        xsp[h, :, w_a] = (
            f32(xb[h, 1, :, w_a]) + f32(part[h, 1, KEEP, w_a]) + f32(x1p[h])
        ).astype(BF16)
        xsp[h, :, w_b] = (f32(xb[h, 1, :, w_b]) + f32(part[h, 1, KEEP, w_b])).astype(BF16)
        s["x2p"] = send(xsp.at[h], x2p.at[h], up)
        s["xhop", 2].wait_recv()
        s["x1m"].wait_recv()
        xsm[h, :, w_a] = (f32(xb[h, 2, :, w_a]) + f32(part[h, 2, KEEP, w_a])).astype(BF16)
        xsm[h, :, w_b] = (
            f32(xb[h, 2, :, w_b]) + f32(part[h, 2, KEEP, w_b]) + f32(x1m[h])
        ).astype(BF16)
        s["x2m"] = send(xsm.at[h], x2m.at[h], down)

    def zsum(h, g):
        s, at = rs[h], pair[g]
        for name in ("plain_p", "plain_m", "sum_p", "sum_m"):
            s[name, g].wait_recv()
        return f32(part[h, 3, at, r_z]) + f32(z2p[h, at]) + f32(z2m[h, at])

    def z_given(h):
        xs[h] = zsum(h, 0).astype(BF16)
        rs[h]["xs"] = send(xs.at[h], xr.at[h], twin)
        xhop(h, 3)

    def lanes(h):
        return pl.ds(h * WIDE, WIDE)

    def z_done(h):
        s = rs[h]
        value = zsum(h, 1)
        s["xs"].wait_recv()
        value = (value + f32(xr[h])).astype(BF16)
        give[r_z, lanes(h)] = value[1]
        s["give_z"] = send(give.at[r_z, lanes(h)], got.at[r_z, lanes(h)], cross)
        kept[r_z, lanes(h)] = value[0]

    def x_done(h):
        s = rs[h]
        for name in (("xhop", 3), "x2p", "x2m"):
            s[name].wait_recv()
        value = (
            f32(xb[h, 3]) + f32(part[h, 3, KEEP, r_x]) + f32(x2p[h]) + f32(x2m[h])
        ).astype(BF16)
        give[r_x, lanes(h)] = value[1]
        s["give_x"] = send(give.at[r_x, lanes(h)], got.at[r_x, lanes(h)], cross)
        kept[r_x, lanes(h)] = value[0]

    def reduce_start(h):
        xhop(h, 0)
        hop(h, 0)
        hop(h, 1)
        xhop(h, 1)
        plain(h, 0)
        xhop(h, 2)

    def reduce_early(h):
        sums(h, 0)
        x_first(h)
        plain(h, 1)
        sums(h, 1)

    def weight_1():
        return [send(gw.at[:, (row + j) % 8], ar1.at[j - 1], others_r[j - 1]) for j in range(1, 8)]

    def weight_2(copies):
        for c in copies:
            c.wait_recv()
        acc = f32(gw[:, row])
        for j in range(7):
            acc = acc + f32(ar1[j])
        for s in range(8):
            ar2s[s] = acc[:, s * 8 : s * 8 + 8, :]
        return [send(ar2s.at[(col + j) % 8], ar2.at[j - 1], others_c[j - 1]) for j in range(1, 8)]

    def weight_3(copies):
        for c in copies:
            c.wait_recv()
        done = ar2s[col]
        for j in range(7):
            done = done + ar2[j]
        ar3[col] = done
        return [send(ar3.at[col], ar3.at[col], others_c[j]) for j in range(7)]

    def weight_4(copies):
        for c in copies:
            c.wait_recv()
        for s in range(8):
            total_gw[:, s * 8 : s * 8 + 8, :] = ar3[s]
        ar4[row] = total_gw[...].astype(BF16)
        return [send(ar4.at[row], ar4.at[row], others_r[j]) for j in range(7)]

    def weight_end(copies):
        for c in copies:
            c.wait_recv()
        for r in range(8):
            for f in range(2):
                grad_weight[r * 64 : r * 64 + 64, f * 256 : f * 256 + 256] = f32(ar4[r, f])

    zero = jnp.zeros((TILE, WIDE), F32)
    run = products(0, 0, 4, zero)
    gather_far(1)
    run = products(0, 4, 8, run)
    gather_near(1)
    products(0, 8, 13, run)
    gather_last(1)
    collect(0)
    reduce_start(0)
    for c in swap:
        c.wait_recv()
    term(lambda: other[0], lambda: other[1], 1 - feat)
    wc = weight_1()
    gather_end(1)
    run = products(1, 0, 2, zero)
    reduce_early(0)
    run = products(1, 2, 6, run)
    wc = weight_2(wc)
    z_given(0)
    x_second(0)
    run = products(1, 6, 10, run)
    wc = weight_3(wc)
    z_done(0)
    products(1, 10, 13, run)
    collect(1)
    reduce_start(1)
    x_done(0)
    wc = weight_4(wc)
    reduce_early(1)
    z_given(1)
    x_second(1)
    z_done(1)
    weight_end(wc)
    x_done(1)

    w_own = pl.ds(pl.multiple_of(feat * 256, 256), 256)
    w_other = pl.ds(pl.multiple_of((1 - feat) * 256, 256), 256)

    def finish(at_rows):
        def columns(n, _):
            at = pl.ds(pl.multiple_of(n * 256, 256), 256)
            dims = (((1,), (1,)), ((), ()))
            value = lax.dot_general(kept[at_rows], weight[at, w_own], dims, preferred_element_type=F32)
            value += lax.dot_general(got[at_rows], weight[at, w_other], dims, preferred_element_type=F32)
            grad_in[at_rows, at] = value.astype(BF16)
            return 0

        lax.fori_loop(0, 4, columns, 0)

    for h in range(2):
        rs[h]["give_z"].wait_recv()
    finish(r_z)
    for h in range(2):
        rs[h]["give_x"].wait_recv()
    finish(r_x)
    for c in started:
        c.wait_send()


COPIES = 2 * 11 + 2 + 2 * 23 + 28


def per_device(grad_out, saved_agg, tile_values, tile_rows, tile_cols, tile_counts, weight):
    vmem = pl.BlockSpec(memory_space=pltpu.VMEM)
    smem = pl.BlockSpec(memory_space=pltpu.SMEM)
    anywhere = pl.BlockSpec(memory_space=pl.ANY)
    scratch = [
        ((SLOTS + 1, TILE, TILE), BF16),
        ((64, TILE, WIDE), BF16), ((64, TILE, WIDE), BF16),
        ((FOURS + 1, TILE, WIDE), BF16), ((2, 4, 4, 512, WIDE), BF16),
        ((2, 4, ZH, WIDE), BF16), ((2, 4, ZH, WIDE), BF16),
        ((2, 4, ZR, WIDE), BF16), ((2, 4, ZR, WIDE), BF16),
        ((2, 4, ZH, WIDE), BF16), ((2, 4, ZH, WIDE), BF16),
        ((2, 2, ZR, WIDE), BF16), ((2, 2, ZR, WIDE), BF16),
        ((2, 4, 2, XR, WIDE), BF16),
        ((2, 2, XH, WIDE), BF16), ((2, 2, XH, WIDE), BF16),
        ((2, 2, XR, WIDE), BF16), ((2, 2, XR, WIDE), BF16),
        ((2, 2, XR, WIDE), BF16), ((2, 2, XR, WIDE), BF16), ((2, 2, XR, WIDE), BF16),
        ((512, 256), BF16), ((512, 256), BF16), ((512, 256), BF16),
        ((1024, 512), BF16), ((1024, 512), BF16), ((2, 8, TILE, WIDE), BF16),
        ((2, 8, 64, 256), BF16), ((2, 64, 256), F32),
        ((7, 2, 64, 256), BF16), ((8, 2, 8, 256), F32), ((7, 2, 8, 256), F32),
        ((8, 2, 8, 256), F32), ((8, 2, 64, 256), BF16),
        ((1, PLACES), I32), ((1, TILE), I32),
    ]
    return pl.pallas_call(
        fused_kernel,
        out_shape=(
            jax.ShapeDtypeStruct((512, 1024), BF16),
            jax.ShapeDtypeStruct((512, 512), F32),
        ),
        in_specs=[vmem, vmem, smem] + [anywhere] * 4,
        out_specs=(vmem, vmem),
        scratch_shapes=[pltpu.VMEM(s, t) for s, t in scratch]
        + [pltpu.SMEM((1, PLACES), I32), pltpu.SMEM((1, TILE), I32)]
        + [
            pltpu.SemaphoreType.DMA((COPIES,)),
            pltpu.SemaphoreType.DMA((COPIES,)),
            pltpu.SemaphoreType.DMA((22,)),
        ],
        compiler_params=pltpu.CompilerParams(
            collective_id=0, has_side_effects=True, vmem_limit_bytes=58 * 2**20
        ),
        name="fused",
    )(
        tile_rows[0], tile_cols[0], tile_counts,
        grad_out.reshape(8, TILE, 256), saved_agg, tile_values[0, 0], weight,
    )


def solution(mesh):
    in_specs = (
        P(("row", "col"), "feat"),
        P(("row", "col"), "feat"),
        P("row", "col", None, None, None),
        P("row", "col", None),
        P("row", "col", None),
        P("row", "col"),
        P(),
    )
    out_specs = (P(("row", "col", "feat"), None), P("feat", None))
    return jax.shard_map(
        per_device, mesh=mesh, in_specs=in_specs, out_specs=out_specs, check_vma=False
    )
```

```python
import jax
import jax.numpy as jnp
from jax import lax
from jax.experimental import pallas as pl
from jax.experimental.pallas import tpu as pltpu
from jax.sharding import PartitionSpec as P

MESH = pl.DeviceIdType.MESH
F32 = jnp.float32
BF16 = jnp.bfloat16
I32 = jnp.int32

TILE = 128
ROW_TILES = 64
SLOTS = 640
STEPS = 352
PLACES = 768
UNROLL = (88, 44)
CHUNKS = 16
WIDE = 128

XR = 224
ZR = 288
XH, ZH = XR // 2, ZR // 2
GIVE, KEEP = pl.ds(0, 2), pl.ds(2, 2)


def fused_kernel(
    rows_hbm, cols_hbm, count_hbm, x_hbm, saved_hbm, tiles_hbm,
    hidden, ar4,
    held, panel0, panel1, slots, part,
    z1p, z1m, z2p, z2m, zsp, zsm, xs, xr, xb, x1p, x1m, x2p, x2m, xw, xsp, xsm,
    give, saved, other, gw, ar1, ar2s, ar2, ar3,
    rows_ref, cols_ref, count_ref, table_v, last_v, table, last,
    ssem, rsem, lsem,
):
    row, col, feat = (lax.axis_index(a) for a in ("row", "col", "feat"))
    y, core, x, z = row // 2, row % 2, col // 4, col % 4
    panels = (panel0, panel1)
    y_up = (((y + 1) % 4) * 2 + core, col, feat)
    y_down = (((y + 3) % 4) * 2 + core, col, feat)
    chip_mate = (y * 2 + 1 - core, col, feat)
    mate = (row, col, 1 - feat)
    up, down = (row, x * 4 + (z + 1) % 4, feat), (row, x * 4 + (z + 3) % 4, feat)
    twin = (row, (1 - x) * 4 + z, feat)
    cross = (row, (1 - x) * 4 + z, 1 - feat)
    others_r = [((row + j) % 8, col, feat) for j in range(1, 8)]
    others_c = [(row, (col + j) % 8, feat) for j in range(1, 8)]
    started = []

    def send(src, dst, to):
        i = len(started)
        copy = pltpu.make_async_remote_copy(
            src_ref=src, dst_ref=dst, send_sem=ssem.at[i], recv_sem=rsem.at[i],
            device_id=to, device_id_type=MESH,
        )
        copy.start()
        started.append(copy)
        return copy

    def f32(value):
        return value.astype(F32)

    local = []
    for h in range(2):
        local.append(
            pltpu.make_async_copy(
                x_hbm.at[:, :, pl.ds(h * WIDE, WIDE)], panels[h].at[pl.ds(row * 8, 8)], lsem.at[h]
            )
        )
    tables = [
        pltpu.make_async_copy(rows_hbm, rows_ref, lsem.at[22]),
        pltpu.make_async_copy(cols_hbm, cols_ref, lsem.at[23]),
        pltpu.make_async_copy(count_hbm, count_ref, lsem.at[24]),
    ]
    local.append(pltpu.make_async_copy(saved_hbm, saved, lsem.at[2]))
    each = SLOTS // CHUNKS
    for n in range(CHUNKS):
        at = pl.ds(n * each, each)
        local.append(pltpu.make_async_copy(tiles_hbm.at[at], held.at[at], lsem.at[3 + n]))
    for c in local[:2] + tables + local[2:]:
        c.start()

    barrier = pltpu.get_barrier_semaphore()
    friends = others_r + others_c + [mate, cross]
    for d in friends:
        pl.semaphore_signal(barrier, inc=1, device_id=d, device_id_type=MESH)
    pl.semaphore_wait(barrier, len(friends))

    r_down, r_up, r_far = (((y + k) % 4) * 2 + core for k in (3, 1, 2))

    def shard(h, r, half=None):
        at = pl.ds(r * 8, 8) if half is None else pl.ds(r * 8 + half * 4, 4)
        return panels[h].at[at]

    def pass_on(h, r, to, half=None):
        return send(shard(h, r, half), shard(h, r, half), to)

    ag = ({}, {})

    def gather_first(h):
        a = ag[h]
        a["up0"], a["down1"] = pass_on(h, row, y_up, 0), pass_on(h, row, y_down, 1)
        a["up1"], a["down0"] = pass_on(h, row, y_up, 1), pass_on(h, row, y_down, 0)
        a["core"] = pass_on(h, row, chip_mate)

    def gather_far(h):
        a = ag[h]
        a["up0"].wait_recv()
        a["far0"] = pass_on(h, r_down, y_up, 0)
        a["down1"].wait_recv()
        a["far1"] = pass_on(h, r_up, y_down, 1)

    def gather_near(h):
        a = ag[h]
        a["up1"].wait_recv()
        a["core_d"] = pass_on(h, r_down, chip_mate)
        a["down0"].wait_recv()
        a["core_u"] = pass_on(h, r_up, chip_mate)

    def gather_last(h):
        a = ag[h]
        a["far0"].wait_recv()
        a["core_f0"] = pass_on(h, r_far, chip_mate, 0)
        a["far1"].wait_recv()
        a["core_f1"] = pass_on(h, r_far, chip_mate, 1)

    def gather_end(h):
        for name in ("core", "core_d", "core_u", "core_f0", "core_f1"):
            ag[h][name].wait_recv()

    local[0].wait()
    gather_first(0)
    swap = [send(x_hbm.at[:, :, pl.ds(h * WIDE, WIDE)], other.at[h], mate) for h in range(2)]

    def iota(shape, axis):
        return lax.broadcasted_iota(I32, shape, axis)

    def total(mask, value, axis):
        return jnp.sum(jnp.where(mask, value, 0), axis=axis, keepdims=True)

    for c in tables:
        c.wait()
    count = count_ref[...]
    slot_r = iota((1, SLOTS), 1)
    slot_c = iota((SLOTS, 1), 0)
    eye = iota((SLOTS, SLOTS), 0) == iota((SLOTS, SLOTS), 1)
    rows_r = jnp.where(slot_r < count, rows_ref[...], ROW_TILES)
    rows_c = total(eye, rows_r, 1)
    cols_c = total(eye, cols_ref[...], 1)
    tile_r, tile_c = iota((1, TILE), 1), iota((TILE, 1), 0)
    n_c = total(rows_r == tile_c, 1, 1)
    n_r = total(rows_c == tile_r, 1, 0)
    n_c = jnp.where(tile_c < ROW_TILES, (n_c + 1) >> 1, 0)
    n_r = jnp.where(tile_r < ROW_TILES, (n_r + 1) >> 1, 0)
    end_r = total(tile_c <= tile_r, n_c, 0)
    start_r = end_r - n_r
    before = total((rows_r == rows_c) & (slot_r < slot_c), 1, 1)
    first = total(rows_c == tile_r, start_r, 1)
    place = jnp.where(rows_c < ROW_TILES, first * 2 + before, PLACES)
    at_r = iota((1, PLACES), 1)
    empty = SLOTS * 64
    word = total(place == at_r, slot_c * 64 + cols_c - empty, 0) + empty
    start_c = total(tile_c == tile_r, start_r, 1)
    opens = total((start_c * 2 == at_r) & (n_c > 0), 1, 0)
    table_v[...] = word + opens * 65536
    last_v[...] = jnp.where(n_r > 0, end_r - 1, STEPS)
    fill = [
        pltpu.make_async_copy(table_v, table, lsem.at[20]),
        pltpu.make_async_copy(last_v, last, lsem.at[21]),
    ]
    for c in fill:
        c.start()

    gather_far(0)
    local[1].wait()
    gather_first(1)

    def term(low, high, slot):
        def columns(n, _):
            at = pl.ds(pl.multiple_of(n * 128, 128), 128)
            source = jnp.concatenate([low().reshape(8 * TILE, WIDE), high().reshape(8 * TILE, WIDE)], axis=1)
            value = lax.dot_general(
                saved[:, at], source, (((0,), (0,)), ((), ())), preferred_element_type=F32
            )
            gw[slot, pl.ds(n * 2, 2)] = value.astype(BF16).reshape(2, 64, 256)
            return 0

        lax.fori_loop(0, 4, columns, 0)

    local[2].wait()
    mine = pl.ds(row * 8, 8)
    term(lambda: panel0[mine], lambda: panel1[mine], feat)
    gather_near(0)
    held[SLOTS] = jnp.zeros((TILE, TILE), BF16)
    slots[STEPS] = jnp.zeros((TILE, WIDE), BF16)
    for c in local[3:] + fill:
        c.wait()
    gather_last(0)
    gather_end(0)

    def products(h, lo, hi, sums):
        panel = panels[h]

        def group(g, sums):
            for u in range(UNROLL[h]):
                p = g * UNROLL[h] + u
                w = [table[0, 2 * p + i] for i in range(2)]
                left = jnp.concatenate([held[(a >> 6) & 1023] for a in w], axis=1)
                right = jnp.concatenate([panel[a & 63] for a in w], axis=0)
                fresh = jnp.dot(left, right, preferred_element_type=F32)
                sums = fresh + jnp.where((w[0] >> 16) > 0, 0.0, sums)
                slots[p] = sums.astype(BF16)
            return sums

        return lax.fori_loop(lo, hi, group, sums)

    quarters = ((1 - x, feat), (x, 1 - feat), (x, feat), (1 - x, 1 - feat))
    offsets = (2, 1, 3, 0)

    def collect(h):
        for o in range(4):
            for q in range(4):
                xx, half = quarters[q]
                base = (xx * 4 + (z + offsets[o]) % 4) * 8 + half * 4
                for t in range(4):
                    part[h, o, q, t * TILE : (t + 1) * TILE] = slots[last[0, base + t]]

    r_x, r_z = pl.ds(0, XR), pl.ds(XR, ZR)
    r_a, r_b = pl.ds(XR, ZH), pl.ds(XR + ZH, ZH)
    v_a, v_b = pl.ds(0, ZH), pl.ds(ZH, ZH)
    w_a, w_b = pl.ds(0, XH), pl.ds(XH, XH)
    rs = ({}, {})
    pair = (GIVE, KEEP)

    def xhop(h, o):
        rs[h]["xhop", o] = send(part.at[h, o, GIVE, r_x], xb.at[h, o], twin)

    def xhop_own(h):
        for k in (1, 0):
            rs[h]["xhop", 3, k] = send(part.at[h, 3, k, r_x], xb.at[h, 3, k], twin)

    def hop(h, g):
        s, at = rs[h], pair[g]
        s["hop_p", g] = send(part.at[h, 0, at, r_a], z1p.at[h, at], up)
        s["hop_m", g] = send(part.at[h, 0, at, r_b], z1m.at[h, at], down)

    def plain(h, g):
        s, at = rs[h], pair[g]
        s["plain_p", g] = send(part.at[h, 1, at, r_b], z2p.at[h, at, v_b], up)
        s["plain_m", g] = send(part.at[h, 2, at, r_a], z2m.at[h, at, v_a], down)

    def sums(h, g):
        s, at = rs[h], pair[g]
        s["hop_p", g].wait_recv()
        zsp[h, at] = (f32(z1p[h, at]) + f32(part[h, 1, at, r_a])).astype(BF16)
        s["sum_p", g] = send(zsp.at[h, at], z2p.at[h, at, v_a], up)
        s["hop_m", g].wait_recv()
        zsm[h, at] = (f32(z1m[h, at]) + f32(part[h, 2, at, r_b])).astype(BF16)
        s["sum_m", g] = send(zsm.at[h, at], z2m.at[h, at, v_b], down)

    def x_first(h):
        s = rs[h]
        s["xhop", 0].wait_recv()
        xw[h] = (f32(xb[h, 0]) + f32(part[h, 0, KEEP, r_x])).astype(BF16)
        s["x1p"] = send(xw.at[h, :, w_a], x1p.at[h], up)
        s["x1m"] = send(xw.at[h, :, w_b], x1m.at[h], down)

    def x_second(h):
        s = rs[h]
        s["xhop", 1].wait_recv()
        s["x1p"].wait_recv()
        xsp[h, :, w_a] = (
            f32(xb[h, 1, :, w_a]) + f32(part[h, 1, KEEP, w_a]) + f32(x1p[h])
        ).astype(BF16)
        xsp[h, :, w_b] = (f32(xb[h, 1, :, w_b]) + f32(part[h, 1, KEEP, w_b])).astype(BF16)
        s["xhop", 2].wait_recv()
        s["x1m"].wait_recv()
        xsm[h, :, w_a] = (f32(xb[h, 2, :, w_a]) + f32(part[h, 2, KEEP, w_a])).astype(BF16)
        xsm[h, :, w_b] = (
            f32(xb[h, 2, :, w_b]) + f32(part[h, 2, KEEP, w_b]) + f32(x1m[h])
        ).astype(BF16)
        for k in (1, 0):
            s["x2p", k] = send(xsp.at[h, k], x2p.at[h, k], up)
            s["x2m", k] = send(xsm.at[h, k], x2m.at[h, k], down)

    def zsum(h, g):
        s, at = rs[h], pair[g]
        for name in ("plain_p", "plain_m", "sum_p", "sum_m"):
            s[name, g].wait_recv()
        return f32(part[h, 3, at, r_z]) + f32(z2p[h, at]) + f32(z2m[h, at])

    def z_given(h):
        xs[h] = zsum(h, 0).astype(BF16)
        rs[h]["xs"] = send(xs.at[h], xr.at[h], twin)
        xhop_own(h)

    def lanes(h):
        return pl.ds(h * WIDE, WIDE)

    def features(h):
        return pl.ds(pl.multiple_of(feat * 256 + h * WIDE, WIDE), WIDE)

    def z_done(h):
        s = rs[h]
        value = zsum(h, 1)
        s["xs"].wait_recv()
        value = (value + f32(xr[h])).astype(BF16)
        give[r_z, lanes(h)] = value[1]
        s["give_z"] = send(give.at[r_z, lanes(h)], hidden.at[r_z, features(h)], cross)
        hidden[r_z, features(h)] = value[0]

    def x_done(h):
        s = rs[h]
        for k in (1, 0):
            for name in (("xhop", 3, k), ("x2p", k), ("x2m", k)):
                s[name].wait_recv()
            value = (
                f32(xb[h, 3, k]) + f32(part[h, 3, 2 + k, r_x]) + f32(x2p[h, k]) + f32(x2m[h, k])
            ).astype(BF16)
            if k == 1:
                give[r_x, lanes(h)] = value
                s["give_x"] = send(give.at[r_x, lanes(h)], hidden.at[r_x, features(h)], cross)
            else:
                hidden[r_x, features(h)] = value

    def reduce_start(h):
        xhop(h, 0)
        hop(h, 0)
        hop(h, 1)
        xhop(h, 1)
        plain(h, 0)
        xhop(h, 2)

    def reduce_early(h):
        x_first(h)
        plain(h, 1)
        sums(h, 1)

    def weight_1():
        return [send(gw.at[:, (col + j) % 8], ar1.at[j - 1], others_c[j - 1]) for j in range(1, 8)]

    def weight_2(copies):
        for c in copies:
            c.wait_recv()
        acc = f32(gw[:, col])
        for j in range(7):
            acc = acc + f32(ar1[j])
        for r in range(8):
            ar2s[r] = acc[:, r * 8 : r * 8 + 8, :]
        return [send(ar2s.at[(row + j) % 8], ar2.at[j - 1], others_r[j - 1]) for j in range(1, 8)]

    def weight_3(copies):
        for c in copies:
            c.wait_recv()
        done = ar2s[row]
        for j in range(7):
            done = done + ar2[j]
        ar3[col] = done.reshape(16, 256).astype(BF16)
        return [send(ar3.at[col], ar3.at[col], others_c[j]) for j in range(7)]

    def weight_4(copies):
        for c in copies:
            c.wait_recv()
        ar4[row] = ar3[...]
        return [send(ar3, ar4.at[row], others_r[j]) for j in range(7)]

    zero = jnp.zeros((TILE, WIDE), F32)
    gather_far(1)
    for c in swap:
        c.wait_recv()
    term(lambda: other[0], lambda: other[1], 1 - feat)
    wc = weight_1()
    run = products(0, 0, 2, zero)
    gather_near(1)
    products(0, 2, 4, run)
    gather_last(1)
    collect(0)
    reduce_start(0)
    wc = weight_2(wc)
    gather_end(1)
    run = products(1, 0, 2, zero)
    sums(0, 0)
    run = products(1, 2, 4, run)
    reduce_early(0)
    run = products(1, 4, 6, run)
    wc = weight_3(wc)
    z_given(0)
    products(1, 6, 8, run)
    x_second(0)
    collect(1)
    reduce_start(1)
    wc = weight_4(wc)
    z_done(0)
    x_done(0)
    sums(1, 0)
    reduce_early(1)
    z_given(1)
    x_second(1)
    z_done(1)
    for c in wc:
        c.wait_recv()
    x_done(1)
    for h in range(2):
        rs[h]["give_z"].wait_recv()
        rs[h]["give_x"].wait_recv()
    for c in started:
        c.wait_send()


def finish_kernel(hidden, weight, pieces, grad_in, grad_weight):
    dims = (((1,), (1,)), ((), ()))
    grad_in[...] = lax.dot_general(
        hidden[...], weight[...], dims, preferred_element_type=F32
    ).astype(BF16)
    for s in range(2):
        for r in range(8):
            piece = pieces[r, s].astype(F32)
            at = s * 64 + r * 8
            for f in range(2):
                grad_weight[at : at + 8, f * 256 : f * 256 + 256] = piece[f * 8 : f * 8 + 8]


def finish(hidden, weight, pieces):
    return pl.pallas_call(
        finish_kernel,
        grid=(4,),
        in_specs=[
            pl.BlockSpec((512, 512), lambda n: (0, 0)),
            pl.BlockSpec((256, 512), lambda n: (n, 0)),
            pl.BlockSpec((8, 2, 16, 256), lambda n: (0, n, 0, 0)),
        ],
        out_specs=(
            pl.BlockSpec((512, 256), lambda n: (0, n)),
            pl.BlockSpec((128, 512), lambda n: (n, 0)),
        ),
        out_shape=(
            jax.ShapeDtypeStruct((512, 1024), BF16),
            jax.ShapeDtypeStruct((512, 512), F32),
        ),
        compiler_params=pltpu.CompilerParams(vmem_limit_bytes=60 * 2**20),
        name="finish",
    )(hidden, weight, pieces)


COPIES = 2 * 11 + 2 + 2 * 26 + 28


def per_device(grad_out, saved_agg, tile_values, tile_rows, tile_cols, tile_counts, weight):
    vmem = pl.BlockSpec(memory_space=pltpu.VMEM)
    anywhere = pl.BlockSpec(memory_space=pl.ANY)
    scratch = [
        ((SLOTS + 1, TILE, TILE), BF16),
        ((64, TILE, WIDE), BF16), ((64, TILE, WIDE), BF16),
        ((STEPS + 1, TILE, WIDE), BF16), ((2, 4, 4, 512, WIDE), BF16),
        ((2, 4, ZH, WIDE), BF16), ((2, 4, ZH, WIDE), BF16),
        ((2, 4, ZR, WIDE), BF16), ((2, 4, ZR, WIDE), BF16),
        ((2, 4, ZH, WIDE), BF16), ((2, 4, ZH, WIDE), BF16),
        ((2, 2, ZR, WIDE), BF16), ((2, 2, ZR, WIDE), BF16),
        ((2, 4, 2, XR, WIDE), BF16),
        ((2, 2, XH, WIDE), BF16), ((2, 2, XH, WIDE), BF16),
        ((2, 2, XR, WIDE), BF16), ((2, 2, XR, WIDE), BF16),
        ((2, 2, XR, WIDE), BF16), ((2, 2, XR, WIDE), BF16), ((2, 2, XR, WIDE), BF16),
        ((512, 256), BF16), ((1024, 512), BF16), ((2, 8, TILE, WIDE), BF16),
        ((2, 8, 64, 256), BF16),
        ((7, 2, 64, 256), BF16), ((8, 2, 8, 256), F32), ((7, 2, 8, 256), F32),
        ((8, 16, 256), BF16),
        ((1, SLOTS), I32), ((1, SLOTS), I32), ((1, 1), I32), ((1, PLACES), I32), ((1, TILE), I32),
    ]
    hidden, pieces = pl.pallas_call(
        fused_kernel,
        out_shape=(
            jax.ShapeDtypeStruct((512, 512), BF16),
            jax.ShapeDtypeStruct((8, 8, 16, 256), BF16),
        ),
        in_specs=[anywhere] * 6,
        out_specs=(vmem, vmem),
        scratch_shapes=[pltpu.VMEM(s, t) for s, t in scratch]
        + [pltpu.SMEM((1, PLACES), I32), pltpu.SMEM((1, TILE), I32)]
        + [
            pltpu.SemaphoreType.DMA((COPIES,)),
            pltpu.SemaphoreType.DMA((COPIES,)),
            pltpu.SemaphoreType.DMA((25,)),
        ],
        compiler_params=pltpu.CompilerParams(
            collective_id=0, has_side_effects=True, vmem_limit_bytes=56 * 2**20
        ),
        name="fused",
    )(
        tile_rows[0], tile_cols[0], tile_counts,
        grad_out.reshape(8, TILE, 256), saved_agg, tile_values[0, 0],
    )
    return finish(hidden, weight, pieces)


def solution(mesh):
    in_specs = (
        P(("row", "col"), "feat"),
        P(("row", "col"), "feat"),
        P("row", "col", None, None, None),
        P("row", "col", None),
        P("row", "col", None),
        P("row", "col"),
        P(),
    )
    out_specs = (P(("row", "col", "feat"), None), P("feat", None))
    return jax.shard_map(
        per_device, mesh=mesh, in_specs=in_specs, out_specs=out_specs, check_vma=False
    )
```

```python
import jax
import jax.numpy as jnp
from jax import lax
from jax.experimental import pallas as pl
from jax.experimental.pallas import tpu as pltpu
from jax.sharding import PartitionSpec as P

MESH = pl.DeviceIdType.MESH
F32 = jnp.float32
BF16 = jnp.bfloat16
I32 = jnp.int32

TILE = 128
ROW_TILES = 64
SLOTS = 640
STEPS = 352
PLACES = 768
UNROLL = (88, 44)
CHUNKS = 16
WIDE = 128

XR = 224
ZR = 288
XH, ZH = XR // 2, ZR // 2
GIVE, KEEP = pl.ds(0, 2), pl.ds(2, 2)


def fused_kernel(
    rows_hbm, cols_hbm, count_hbm, x_hbm, saved_hbm, tiles_hbm,
    hidden_hbm, pieces_hbm,
    held, panel0, panel1, slots, part,
    z1p, z1m, z2p, z2m, zsp, zsm, xs, xr, xb, x1p, x1m, x2p, x2m, xw, xsp, xsm,
    give, hidden, saved, other, gw, ar1, ar2s, ar2, ar3, ar4,
    rows_ref, cols_ref, count_ref, table_v, last_v, table, last,
    ssem, rsem, lsem,
):
    row, col, feat = (lax.axis_index(a) for a in ("row", "col", "feat"))
    y, core, x, z = row // 2, row % 2, col // 4, col % 4
    panels = (panel0, panel1)
    y_up = (((y + 1) % 4) * 2 + core, col, feat)
    y_down = (((y + 3) % 4) * 2 + core, col, feat)
    chip_mate = (y * 2 + 1 - core, col, feat)
    mate = (row, col, 1 - feat)
    up, down = (row, x * 4 + (z + 1) % 4, feat), (row, x * 4 + (z + 3) % 4, feat)
    twin = (row, (1 - x) * 4 + z, feat)
    cross = (row, (1 - x) * 4 + z, 1 - feat)
    others_r = [((row + j) % 8, col, feat) for j in range(1, 8)]
    others_c = [(row, (col + j) % 8, feat) for j in range(1, 8)]
    started = []

    def send(src, dst, to):
        i = len(started)
        copy = pltpu.make_async_remote_copy(
            src_ref=src, dst_ref=dst, send_sem=ssem.at[i], recv_sem=rsem.at[i],
            device_id=to, device_id_type=MESH,
        )
        copy.start()
        started.append(copy)
        return copy

    def f32(value):
        return value.astype(F32)

    barrier = pltpu.get_barrier_semaphore()
    friends = others_r + others_c + [mate, cross]
    for d in friends:
        pl.semaphore_signal(barrier, inc=1, device_id=d, device_id_type=MESH)

    local = []
    for h in range(2):
        local.append(
            pltpu.make_async_copy(
                x_hbm.at[:, :, pl.ds(h * WIDE, WIDE)], panels[h].at[pl.ds(row * 8, 8)], lsem.at[h]
            )
        )
    tables = [
        pltpu.make_async_copy(rows_hbm, rows_ref, lsem.at[22]),
        pltpu.make_async_copy(cols_hbm, cols_ref, lsem.at[23]),
        pltpu.make_async_copy(count_hbm, count_ref, lsem.at[24]),
    ]
    local.append(pltpu.make_async_copy(saved_hbm, saved, lsem.at[2]))
    each = SLOTS // CHUNKS
    for n in range(CHUNKS):
        at = pl.ds(n * each, each)
        local.append(pltpu.make_async_copy(tiles_hbm.at[at], held.at[at], lsem.at[3 + n]))
    for c in local[:2] + tables + local[2:]:
        c.start()
    pl.semaphore_wait(barrier, len(friends))

    r_down, r_up, r_far = (((y + k) % 4) * 2 + core for k in (3, 1, 2))

    def shard(h, r, half=None):
        at = pl.ds(r * 8, 8) if half is None else pl.ds(r * 8 + half * 4, 4)
        return panels[h].at[at]

    def pass_on(h, r, to, half=None):
        return send(shard(h, r, half), shard(h, r, half), to)

    ag = ({}, {})

    def gather_first(h):
        a = ag[h]
        a["up0"], a["down1"] = pass_on(h, row, y_up, 0), pass_on(h, row, y_down, 1)
        a["up1"], a["down0"] = pass_on(h, row, y_up, 1), pass_on(h, row, y_down, 0)
        a["core"] = pass_on(h, row, chip_mate)

    def gather_far(h):
        a = ag[h]
        a["up0"].wait_recv()
        a["far0"] = pass_on(h, r_down, y_up, 0)
        a["down1"].wait_recv()
        a["far1"] = pass_on(h, r_up, y_down, 1)

    def gather_near(h):
        a = ag[h]
        a["up1"].wait_recv()
        a["core_d"] = pass_on(h, r_down, chip_mate)
        a["down0"].wait_recv()
        a["core_u"] = pass_on(h, r_up, chip_mate)

    def gather_last(h):
        a = ag[h]
        a["far0"].wait_recv()
        a["core_f0"] = pass_on(h, r_far, chip_mate, 0)
        a["far1"].wait_recv()
        a["core_f1"] = pass_on(h, r_far, chip_mate, 1)

    def gather_end(h):
        for name in ("core", "core_d", "core_u", "core_f0", "core_f1"):
            ag[h][name].wait_recv()

    local[0].wait()
    gather_first(0)
    swap = [send(x_hbm.at[:, :, pl.ds(h * WIDE, WIDE)], other.at[h], mate) for h in range(2)]

    def iota(shape, axis):
        return lax.broadcasted_iota(I32, shape, axis)

    def total(mask, value, axis):
        return jnp.sum(jnp.where(mask, value, 0), axis=axis, keepdims=True)

    for c in tables:
        c.wait()
    count = count_ref[...]
    slot_r = iota((1, SLOTS), 1)
    slot_c = iota((SLOTS, 1), 0)
    eye = iota((SLOTS, SLOTS), 0) == iota((SLOTS, SLOTS), 1)
    rows_r = jnp.where(slot_r < count, rows_ref[...], ROW_TILES)
    rows_c = total(eye, rows_r, 1)
    cols_c = total(eye, cols_ref[...], 1)
    tile_r, tile_c = iota((1, TILE), 1), iota((TILE, 1), 0)
    n_c = total(rows_r == tile_c, 1, 1)
    n_r = total(rows_c == tile_r, 1, 0)
    n_c = jnp.where(tile_c < ROW_TILES, (n_c + 1) >> 1, 0)
    n_r = jnp.where(tile_r < ROW_TILES, (n_r + 1) >> 1, 0)
    end_r = total(tile_c <= tile_r, n_c, 0)
    start_r = end_r - n_r
    before = total((rows_r == rows_c) & (slot_r < slot_c), 1, 1)
    first = total(rows_c == tile_r, start_r, 1)
    place = jnp.where(rows_c < ROW_TILES, first * 2 + before, PLACES)
    at_r = iota((1, PLACES), 1)
    empty = SLOTS * 64
    word = total(place == at_r, slot_c * 64 + cols_c - empty, 0) + empty
    start_c = total(tile_c == tile_r, start_r, 1)
    opens = total((start_c * 2 == at_r) & (n_c > 0), 1, 0)
    table_v[...] = word + opens * 65536
    last_v[...] = jnp.where(n_r > 0, end_r - 1, STEPS)
    fill = [
        pltpu.make_async_copy(table_v, table, lsem.at[20]),
        pltpu.make_async_copy(last_v, last, lsem.at[21]),
    ]
    for c in fill:
        c.start()

    gather_far(0)
    local[1].wait()
    gather_first(1)

    def term(low, high, slot):
        def columns(n, _):
            at = pl.ds(pl.multiple_of(n * 128, 128), 128)
            source = jnp.concatenate([low().reshape(8 * TILE, WIDE), high().reshape(8 * TILE, WIDE)], axis=1)
            value = lax.dot_general(
                saved[:, at], source, (((0,), (0,)), ((), ())), preferred_element_type=F32
            )
            gw[slot, pl.ds(n * 2, 2)] = value.astype(BF16).reshape(2, 64, 256)
            return 0

        lax.fori_loop(0, 4, columns, 0)

    local[2].wait()
    mine = pl.ds(row * 8, 8)
    term(lambda: panel0[mine], lambda: panel1[mine], feat)
    gather_near(0)
    held[SLOTS] = jnp.zeros((TILE, TILE), BF16)
    slots[STEPS] = jnp.zeros((TILE, WIDE), BF16)
    for c in local[3:] + fill:
        c.wait()
    gather_last(0)
    gather_end(0)

    def products(h, lo, hi, sums):
        panel = panels[h]

        def group(g, sums):
            for u in range(UNROLL[h]):
                p = g * UNROLL[h] + u
                w = [table[0, 2 * p + i] for i in range(2)]
                left = jnp.concatenate([held[(a >> 6) & 1023] for a in w], axis=1)
                right = jnp.concatenate([panel[a & 63] for a in w], axis=0)
                fresh = jnp.dot(left, right, preferred_element_type=F32)
                sums = fresh + jnp.where((w[0] >> 16) > 0, 0.0, sums)
                slots[p] = sums.astype(BF16)
            return sums

        return lax.fori_loop(lo, hi, group, sums)

    quarters = ((1 - x, feat), (x, 1 - feat), (x, feat), (1 - x, 1 - feat))
    offsets = (2, 1, 3, 0)

    def collect(h, first, end):
        for o in range(first, end):
            for q in range(4):
                xx, half = quarters[q]
                base = (xx * 4 + (z + offsets[o]) % 4) * 8 + half * 4
                for t in range(4):
                    part[h, o, q, t * TILE : (t + 1) * TILE] = slots[last[0, base + t]]

    r_x, r_z = pl.ds(0, XR), pl.ds(XR, ZR)
    r_a, r_b = pl.ds(XR, ZH), pl.ds(XR + ZH, ZH)
    v_a, v_b = pl.ds(0, ZH), pl.ds(ZH, ZH)
    w_a, w_b = pl.ds(0, XH), pl.ds(XH, XH)
    rs = ({}, {})
    pair = (GIVE, KEEP)

    def xhop(h, o):
        rs[h]["xhop", o] = send(part.at[h, o, GIVE, r_x], xb.at[h, o], twin)

    def xhop_own(h):
        for k in (1, 0):
            rs[h]["xhop", 3, k] = send(part.at[h, 3, k, r_x], xb.at[h, 3, k], twin)

    def hop(h, g):
        s, at = rs[h], pair[g]
        s["hop_p", g] = send(part.at[h, 0, at, r_a], z1p.at[h, at], up)
        s["hop_m", g] = send(part.at[h, 0, at, r_b], z1m.at[h, at], down)

    def plain(h, g):
        s, at = rs[h], pair[g]
        s["plain_p", g] = send(part.at[h, 1, at, r_b], z2p.at[h, at, v_b], up)
        s["plain_m", g] = send(part.at[h, 2, at, r_a], z2m.at[h, at, v_a], down)

    def sums(h, g):
        s, at = rs[h], pair[g]
        s["hop_p", g].wait_recv()
        zsp[h, at] = (f32(z1p[h, at]) + f32(part[h, 1, at, r_a])).astype(BF16)
        s["sum_p", g] = send(zsp.at[h, at], z2p.at[h, at, v_a], up)
        s["hop_m", g].wait_recv()
        zsm[h, at] = (f32(z1m[h, at]) + f32(part[h, 2, at, r_b])).astype(BF16)
        s["sum_m", g] = send(zsm.at[h, at], z2m.at[h, at, v_b], down)

    def x_first(h):
        s = rs[h]
        s["xhop", 0].wait_recv()
        xw[h] = (f32(xb[h, 0]) + f32(part[h, 0, KEEP, r_x])).astype(BF16)
        s["x1p"] = send(xw.at[h, :, w_a], x1p.at[h], up)
        s["x1m"] = send(xw.at[h, :, w_b], x1m.at[h], down)

    def x_second(h):
        s = rs[h]
        s["xhop", 1].wait_recv()
        s["x1p"].wait_recv()
        xsp[h, :, w_a] = (
            f32(xb[h, 1, :, w_a]) + f32(part[h, 1, KEEP, w_a]) + f32(x1p[h])
        ).astype(BF16)
        xsp[h, :, w_b] = (f32(xb[h, 1, :, w_b]) + f32(part[h, 1, KEEP, w_b])).astype(BF16)
        s["xhop", 2].wait_recv()
        s["x1m"].wait_recv()
        xsm[h, :, w_a] = (f32(xb[h, 2, :, w_a]) + f32(part[h, 2, KEEP, w_a])).astype(BF16)
        xsm[h, :, w_b] = (
            f32(xb[h, 2, :, w_b]) + f32(part[h, 2, KEEP, w_b]) + f32(x1m[h])
        ).astype(BF16)
        for k in (1, 0):
            s["x2p", k] = send(xsp.at[h, k], x2p.at[h, k], up)
            s["x2m", k] = send(xsm.at[h, k], x2m.at[h, k], down)

    def zsum(h, g):
        s, at = rs[h], pair[g]
        for name in ("plain_p", "plain_m", "sum_p", "sum_m"):
            s[name, g].wait_recv()
        return f32(part[h, 3, at, r_z]) + f32(z2p[h, at]) + f32(z2m[h, at])

    def z_given(h):
        xs[h] = zsum(h, 0).astype(BF16)
        rs[h]["xs"] = send(xs.at[h], xr.at[h], twin)
        xhop_own(h)

    def lanes(h):
        return pl.ds(h * WIDE, WIDE)

    def features(h):
        return pl.ds(pl.multiple_of(feat * 256 + h * WIDE, WIDE), WIDE)

    def z_done(h):
        s = rs[h]
        value = zsum(h, 1)
        s["xs"].wait_recv()
        value = (value + f32(xr[h])).astype(BF16)
        give[r_z, lanes(h)] = value[1]
        s["give_z"] = send(give.at[r_z, lanes(h)], hidden.at[r_z, features(h)], cross)
        hidden[r_z, features(h)] = value[0]

    def x_done(h):
        s = rs[h]
        for k in (1, 0):
            for name in (("xhop", 3, k), ("x2p", k), ("x2m", k)):
                s[name].wait_recv()
            value = (
                f32(xb[h, 3, k]) + f32(part[h, 3, 2 + k, r_x]) + f32(x2p[h, k]) + f32(x2m[h, k])
            ).astype(BF16)
            if k == 1:
                give[r_x, lanes(h)] = value
                s["give_x"] = send(give.at[r_x, lanes(h)], hidden.at[r_x, features(h)], cross)
            else:
                hidden[r_x, features(h)] = value

    def reduce_start(h):
        collect(h, 0, 1)
        xhop(h, 0)
        hop(h, 0)
        hop(h, 1)
        collect(h, 1, 4)
        xhop(h, 1)
        plain(h, 0)
        xhop(h, 2)

    def reduce_early(h):
        x_first(h)
        plain(h, 1)
        sums(h, 1)

    def weight_1():
        return [send(gw.at[:, (col + j) % 8], ar1.at[j - 1], others_c[j - 1]) for j in range(1, 8)]

    def weight_2(copies):
        for c in copies:
            c.wait_recv()
        acc = f32(gw[:, col])
        for j in range(7):
            acc = acc + f32(ar1[j])
        for r in range(8):
            ar2s[r] = acc[:, r * 8 : r * 8 + 8, :]
        return [send(ar2s.at[(row + j) % 8], ar2.at[j - 1], others_r[j - 1]) for j in range(1, 8)]

    def weight_3(copies):
        for c in copies:
            c.wait_recv()
        done = ar2s[row]
        for j in range(7):
            done = done + ar2[j]
        ar3[col] = done.reshape(16, 256).astype(BF16)
        return [send(ar3.at[col], ar3.at[col], others_c[j]) for j in range(7)]

    def weight_4(copies):
        for c in copies:
            c.wait_recv()
        ar4[row] = ar3[...]
        return [send(ar3, ar4.at[row], others_r[j]) for j in range(7)]

    zero = jnp.zeros((TILE, WIDE), F32)
    gather_far(1)
    for c in swap:
        c.wait_recv()
    term(lambda: other[0], lambda: other[1], 1 - feat)
    wc = weight_1()
    run = products(0, 0, 2, zero)
    gather_near(1)
    products(0, 2, 4, run)
    gather_last(1)
    reduce_start(0)
    wc = weight_2(wc)
    gather_end(1)
    run = products(1, 0, 2, zero)
    sums(0, 0)
    run = products(1, 2, 4, run)
    reduce_early(0)
    run = products(1, 4, 6, run)
    wc = weight_3(wc)
    z_given(0)
    products(1, 6, 8, run)
    x_second(0)
    reduce_start(1)
    wc = weight_4(wc)
    z_done(0)
    x_done(0)
    sums(1, 0)
    reduce_early(1)
    z_given(1)
    x_second(1)
    z_done(1)
    for c in wc:
        c.wait_recv()
    out = [pltpu.make_async_copy(ar4, pieces_hbm, lsem.at[0])]
    out[0].start()
    x_done(1)
    for at, name in ((r_z, "give_z"), (r_x, "give_x")):
        for h in range(2):
            rs[h][name].wait_recv()
        out.append(pltpu.make_async_copy(hidden.at[at], hidden_hbm.at[at], lsem.at[len(out)]))
        out[-1].start()
    for c in out:
        c.wait()
    for c in started:
        c.wait_send()


def finish_kernel(
    hidden, weight, pieces, grad_in, grad_weight, hidden_v, weight_v, pieces_v, left, right, sems
):
    copies = [pltpu.make_async_copy(hidden, hidden_v, sems.at[0])]
    blocks = [pl.ds(n * 256, 256) for n in range(4)]
    for n, at in enumerate(blocks):
        copies.append(pltpu.make_async_copy(weight.at[at], weight_v.at[at], sems.at[1 + n]))
    copies.append(pltpu.make_async_copy(pieces, pieces_v, sems.at[5]))
    for c in copies:
        c.start()
    copies[0].wait()
    dims = (((1,), (1,)), ((), ()))
    out = []
    for n, at in enumerate(blocks):
        copies[1 + n].wait()
        left[:, at] = lax.dot_general(
            hidden_v[...], weight_v[at], dims, preferred_element_type=F32
        ).astype(BF16)
        out.append(pltpu.make_async_copy(left.at[:, at], grad_in.at[:, at], sems.at[6 + n]))
        out[-1].start()
        if n == 2:
            copies[5].wait()
            for s in range(8):
                for r in range(8):
                    piece = pieces_v[r, s].astype(F32)
                    rows = s * 64 + r * 8
                    for f in range(2):
                        right[rows : rows + 8, f * 256 : f * 256 + 256] = piece[f * 8 : f * 8 + 8]
            out.append(pltpu.make_async_copy(right, grad_weight, sems.at[10]))
            out[-1].start()
    for c in out:
        c.wait()


def finish(hidden, weight, pieces):
    anywhere = pl.BlockSpec(memory_space=pl.ANY)
    return pl.pallas_call(
        finish_kernel,
        in_specs=[anywhere] * 3,
        out_specs=(anywhere, anywhere),
        out_shape=(
            jax.ShapeDtypeStruct((512, 1024), BF16),
            jax.ShapeDtypeStruct((512, 512), F32),
        ),
        scratch_shapes=[
            pltpu.VMEM((512, 512), BF16),
            pltpu.VMEM((1024, 512), BF16),
            pltpu.VMEM((8, 8, 16, 256), BF16),
            pltpu.VMEM((512, 1024), BF16),
            pltpu.VMEM((512, 512), F32),
            pltpu.SemaphoreType.DMA((11,)),
        ],
        compiler_params=pltpu.CompilerParams(vmem_limit_bytes=60 * 2**20),
        name="finish",
    )(hidden, weight, pieces)


COPIES = 2 * 11 + 2 + 2 * 26 + 28


def per_device(grad_out, saved_agg, tile_values, tile_rows, tile_cols, tile_counts, weight):
    anywhere = pl.BlockSpec(memory_space=pl.ANY)
    scratch = [
        ((SLOTS + 1, TILE, TILE), BF16),
        ((64, TILE, WIDE), BF16), ((64, TILE, WIDE), BF16),
        ((STEPS + 1, TILE, WIDE), BF16), ((2, 4, 4, 512, WIDE), BF16),
        ((2, 4, ZH, WIDE), BF16), ((2, 4, ZH, WIDE), BF16),
        ((2, 4, ZR, WIDE), BF16), ((2, 4, ZR, WIDE), BF16),
        ((2, 4, ZH, WIDE), BF16), ((2, 4, ZH, WIDE), BF16),
        ((2, 2, ZR, WIDE), BF16), ((2, 2, ZR, WIDE), BF16),
        ((2, 4, 2, XR, WIDE), BF16),
        ((2, 2, XH, WIDE), BF16), ((2, 2, XH, WIDE), BF16),
        ((2, 2, XR, WIDE), BF16), ((2, 2, XR, WIDE), BF16),
        ((2, 2, XR, WIDE), BF16), ((2, 2, XR, WIDE), BF16), ((2, 2, XR, WIDE), BF16),
        ((512, 256), BF16), ((512, 512), BF16), ((1024, 512), BF16), ((2, 8, TILE, WIDE), BF16),
        ((2, 8, 64, 256), BF16),
        ((7, 2, 64, 256), BF16), ((8, 2, 8, 256), F32), ((7, 2, 8, 256), F32),
        ((8, 16, 256), BF16), ((8, 8, 16, 256), BF16),
        ((1, SLOTS), I32), ((1, SLOTS), I32), ((1, 1), I32), ((1, PLACES), I32), ((1, TILE), I32),
    ]
    hidden, pieces = pl.pallas_call(
        fused_kernel,
        out_shape=(
            jax.ShapeDtypeStruct((512, 512), BF16),
            jax.ShapeDtypeStruct((8, 8, 16, 256), BF16),
        ),
        in_specs=[anywhere] * 6,
        out_specs=(anywhere, anywhere),
        scratch_shapes=[pltpu.VMEM(s, t) for s, t in scratch]
        + [pltpu.SMEM((1, PLACES), I32), pltpu.SMEM((1, TILE), I32)]
        + [
            pltpu.SemaphoreType.DMA((COPIES,)),
            pltpu.SemaphoreType.DMA((COPIES,)),
            pltpu.SemaphoreType.DMA((25,)),
        ],
        compiler_params=pltpu.CompilerParams(
            collective_id=0, has_side_effects=True, vmem_limit_bytes=56 * 2**20
        ),
        name="fused",
    )(
        tile_rows[0], tile_cols[0], tile_counts,
        grad_out.reshape(8, TILE, 256), saved_agg, tile_values[0, 0],
    )
    return finish(hidden, weight, pieces)


def solution(mesh):
    in_specs = (
        P(("row", "col"), "feat"),
        P(("row", "col"), "feat"),
        P("row", "col", None, None, None),
        P("row", "col", None),
        P("row", "col", None),
        P("row", "col"),
        P(),
    )
    out_specs = (P(("row", "col", "feat"), None), P("feat", None))
    return jax.shard_map(
        per_device, mesh=mesh, in_specs=in_specs, out_specs=out_specs, check_vma=False
    )
```

```python
import jax
import jax.numpy as jnp
from jax import lax
from jax.experimental import pallas as pl
from jax.experimental.pallas import tpu as pltpu
from jax.sharding import PartitionSpec as P

MESH = pl.DeviceIdType.MESH
F32 = jnp.float32
BF16 = jnp.bfloat16
I32 = jnp.int32

TILE = 128
ROW_TILES = 64
SLOTS = 640
STEPS = 352
PLACES = 768
UNROLL = (88, 44)
CHUNKS = 16
WIDE = 128

XR = 224
ZR = 288
XH, ZH = XR // 2, ZR // 2
GIVE, KEEP = pl.ds(0, 2), pl.ds(2, 2)


def fused_kernel(
    rows_hbm, cols_hbm, count_hbm, x_hbm, saved_hbm, tiles_hbm,
    hidden_hbm, pieces_hbm,
    held, panel0, panel1, slots, part,
    z1p, z1m, z2p, z2m, zsp, zsm, xs, xr, xb, x1p, x1m, x2p, x2m, xw, xsp, xsm,
    give, hidden, x_v, saved, other, gw, ar1, ar2s, ar2, ar3, ar4,
    rows_ref, cols_ref, count_ref, table_v, last_v, table, last,
    ssem, rsem, lsem,
):
    row, col, feat = (lax.axis_index(a) for a in ("row", "col", "feat"))
    y, core, x, z = row // 2, row % 2, col // 4, col % 4
    panels = (panel0, panel1)
    y_up = (((y + 1) % 4) * 2 + core, col, feat)
    y_down = (((y + 3) % 4) * 2 + core, col, feat)
    chip_mate = (y * 2 + 1 - core, col, feat)
    mate = (row, col, 1 - feat)
    up, down = (row, x * 4 + (z + 1) % 4, feat), (row, x * 4 + (z + 3) % 4, feat)
    twin = (row, (1 - x) * 4 + z, feat)
    cross = (row, (1 - x) * 4 + z, 1 - feat)
    others_r = [((row + j) % 8, col, feat) for j in range(1, 8)]
    others_c = [(row, (col + j) % 8, feat) for j in range(1, 8)]
    started = []

    def send(src, dst, to):
        i = len(started)
        copy = pltpu.make_async_remote_copy(
            src_ref=src, dst_ref=dst, send_sem=ssem.at[i], recv_sem=rsem.at[i],
            device_id=to, device_id_type=MESH,
        )
        copy.start()
        started.append(copy)
        return copy

    def f32(value):
        return value.astype(F32)

    barrier = pltpu.get_barrier_semaphore()
    friends = others_r + others_c + [mate, cross]
    for d in friends:
        pl.semaphore_signal(barrier, inc=1, device_id=d, device_id_type=MESH)

    local = [
        pltpu.make_async_copy(x_hbm, x_v, lsem.at[0]),
        pltpu.make_async_copy(saved_hbm, saved, lsem.at[1]),
    ]
    tables = [
        pltpu.make_async_copy(rows_hbm, rows_ref, lsem.at[22]),
        pltpu.make_async_copy(cols_hbm, cols_ref, lsem.at[23]),
        pltpu.make_async_copy(count_hbm, count_ref, lsem.at[24]),
    ]
    each = SLOTS // CHUNKS
    for n in range(CHUNKS):
        at = pl.ds(n * each, each)
        local.append(pltpu.make_async_copy(tiles_hbm.at[at], held.at[at], lsem.at[2 + n]))
    for c in local[:1] + tables + local[1:]:
        c.start()
    pl.semaphore_wait(barrier, len(friends))

    r_down, r_up, r_far = (((y + k) % 4) * 2 + core for k in (3, 1, 2))

    def shard(h, r, half=None):
        at = pl.ds(r * 8, 8) if half is None else pl.ds(r * 8 + half * 4, 4)
        return panels[h].at[at]

    def pass_on(h, r, to, half=None):
        return send(shard(h, r, half), shard(h, r, half), to)

    ag = ({}, {})

    def gather_first(h):
        a = ag[h]
        a["up0"], a["down1"] = pass_on(h, row, y_up, 0), pass_on(h, row, y_down, 1)
        a["up1"], a["down0"] = pass_on(h, row, y_up, 1), pass_on(h, row, y_down, 0)
        a["core"] = pass_on(h, row, chip_mate)

    def gather_far(h):
        a = ag[h]
        a["up0"].wait_recv()
        a["far0"] = pass_on(h, r_down, y_up, 0)
        a["down1"].wait_recv()
        a["far1"] = pass_on(h, r_up, y_down, 1)

    def gather_near(h):
        a = ag[h]
        a["up1"].wait_recv()
        a["core_d"] = pass_on(h, r_down, chip_mate)
        a["down0"].wait_recv()
        a["core_u"] = pass_on(h, r_up, chip_mate)

    def gather_last(h):
        a = ag[h]
        a["far0"].wait_recv()
        a["core_f0"] = pass_on(h, r_far, chip_mate, 0)
        a["far1"].wait_recv()
        a["core_f1"] = pass_on(h, r_far, chip_mate, 1)

    def gather_end(h):
        for name in ("core", "core_d", "core_u", "core_f0", "core_f1"):
            ag[h][name].wait_recv()

    mine = pl.ds(row * 8, 8)
    local[0].wait()
    panel0[mine] = x_v[:, :, :WIDE]
    gather_first(0)
    panel1[mine] = x_v[:, :, WIDE:]
    swap = [send(shard(h, row), other.at[h], mate) for h in range(2)]

    def iota(shape, axis):
        return lax.broadcasted_iota(I32, shape, axis)

    def total(mask, value, axis):
        return jnp.sum(jnp.where(mask, value, 0), axis=axis, keepdims=True)

    for c in tables:
        c.wait()
    count = count_ref[...]
    slot_r = iota((1, SLOTS), 1)
    slot_c = iota((SLOTS, 1), 0)
    eye = iota((SLOTS, SLOTS), 0) == iota((SLOTS, SLOTS), 1)
    rows_r = jnp.where(slot_r < count, rows_ref[...], ROW_TILES)
    rows_c = total(eye, rows_r, 1)
    cols_c = total(eye, cols_ref[...], 1)
    tile_r, tile_c = iota((1, TILE), 1), iota((TILE, 1), 0)
    n_c = total(rows_r == tile_c, 1, 1)
    n_r = total(rows_c == tile_r, 1, 0)
    n_c = jnp.where(tile_c < ROW_TILES, (n_c + 1) >> 1, 0)
    n_r = jnp.where(tile_r < ROW_TILES, (n_r + 1) >> 1, 0)
    end_r = total(tile_c <= tile_r, n_c, 0)
    start_r = end_r - n_r
    before = total((rows_r == rows_c) & (slot_r < slot_c), 1, 1)
    first = total(rows_c == tile_r, start_r, 1)
    place = jnp.where(rows_c < ROW_TILES, first * 2 + before, PLACES)
    at_r = iota((1, PLACES), 1)
    empty = SLOTS * 64
    word = total(place == at_r, slot_c * 64 + cols_c - empty, 0) + empty
    start_c = total(tile_c == tile_r, start_r, 1)
    opens = total((start_c * 2 == at_r) & (n_c > 0), 1, 0)
    table_v[...] = word + opens * 65536
    last_v[...] = jnp.where(n_r > 0, end_r - 1, STEPS)
    fill = [
        pltpu.make_async_copy(table_v, table, lsem.at[20]),
        pltpu.make_async_copy(last_v, last, lsem.at[21]),
    ]
    for c in fill:
        c.start()

    gather_far(0)
    gather_first(1)

    def term(low, high, slot):
        def columns(n, _):
            at = pl.ds(pl.multiple_of(n * 128, 128), 128)
            source = jnp.concatenate([low().reshape(8 * TILE, WIDE), high().reshape(8 * TILE, WIDE)], axis=1)
            value = lax.dot_general(
                saved[:, at], source, (((0,), (0,)), ((), ())), preferred_element_type=F32
            )
            gw[slot, pl.ds(n * 2, 2)] = value.astype(BF16).reshape(2, 64, 256)
            return 0

        lax.fori_loop(0, 4, columns, 0)

    local[1].wait()
    term(lambda: panel0[mine], lambda: panel1[mine], feat)
    gather_near(0)
    held[SLOTS] = jnp.zeros((TILE, TILE), BF16)
    slots[STEPS] = jnp.zeros((TILE, WIDE), BF16)
    for c in local[2:] + fill:
        c.wait()
    gather_last(0)
    gather_end(0)

    def products(h, lo, hi, sums):
        panel = panels[h]

        def group(g, sums):
            for u in range(UNROLL[h]):
                p = g * UNROLL[h] + u
                w = [table[0, 2 * p + i] for i in range(2)]
                left = jnp.concatenate([held[(a >> 6) & 1023] for a in w], axis=1)
                right = jnp.concatenate([panel[a & 63] for a in w], axis=0)
                fresh = jnp.dot(left, right, preferred_element_type=F32)
                sums = fresh + jnp.where((w[0] >> 16) > 0, 0.0, sums)
                slots[p] = sums.astype(BF16)
            return sums

        return lax.fori_loop(lo, hi, group, sums)

    quarters = ((1 - x, feat), (x, 1 - feat), (x, feat), (1 - x, 1 - feat))
    offsets = (2, 1, 3, 0)

    def collect(h, first, end):
        for o in range(first, end):
            for q in range(4):
                xx, half = quarters[q]
                base = (xx * 4 + (z + offsets[o]) % 4) * 8 + half * 4
                for t in range(4):
                    part[h, o, q, t * TILE : (t + 1) * TILE] = slots[last[0, base + t]]

    r_x, r_z = pl.ds(0, XR), pl.ds(XR, ZR)
    r_a, r_b = pl.ds(XR, ZH), pl.ds(XR + ZH, ZH)
    v_a, v_b = pl.ds(0, ZH), pl.ds(ZH, ZH)
    w_a, w_b = pl.ds(0, XH), pl.ds(XH, XH)
    rs = ({}, {})
    pair = (GIVE, pl.ds(3, 1), pl.ds(2, 1))

    def xhop(h, o):
        rs[h]["xhop", o] = send(part.at[h, o, GIVE, r_x], xb.at[h, o], twin)

    def hop(h, g):
        s, at = rs[h], pair[g]
        s["hop_p", g] = send(part.at[h, 0, at, r_a], z1p.at[h, at], up)
        s["hop_m", g] = send(part.at[h, 0, at, r_b], z1m.at[h, at], down)

    def plain(h, g):
        s, at = rs[h], pair[g]
        s["plain_p", g] = send(part.at[h, 1, at, r_b], z2p.at[h, at, v_b], up)
        s["plain_m", g] = send(part.at[h, 2, at, r_a], z2m.at[h, at, v_a], down)

    def sums(h, g):
        s, at = rs[h], pair[g]
        s["hop_p", g].wait_recv()
        zsp[h, at] = (f32(z1p[h, at]) + f32(part[h, 1, at, r_a])).astype(BF16)
        s["sum_p", g] = send(zsp.at[h, at], z2p.at[h, at, v_a], up)
        s["hop_m", g].wait_recv()
        zsm[h, at] = (f32(z1m[h, at]) + f32(part[h, 2, at, r_b])).astype(BF16)
        s["sum_m", g] = send(zsm.at[h, at], z2m.at[h, at, v_b], down)

    def x_first(h):
        s = rs[h]
        s["xhop", 0].wait_recv()
        xw[h] = (f32(xb[h, 0]) + f32(part[h, 0, KEEP, r_x])).astype(BF16)
        s["x1p"] = send(xw.at[h, :, w_a], x1p.at[h], up)
        s["x1m"] = send(xw.at[h, :, w_b], x1m.at[h], down)

    def x_second(h, k):
        s = rs[h]
        if k == 1:
            s["xhop", 1].wait_recv()
        if k == 1:
            s["x1p"].wait_recv()
        own = part[h, 1, 2 + k, r_x]
        xsp[h, k, w_a] = (f32(xb[h, 1, k, w_a]) + f32(own[:XH]) + f32(x1p[h, k])).astype(BF16)
        xsp[h, k, w_b] = (f32(xb[h, 1, k, w_b]) + f32(own[XH:])).astype(BF16)
        s["x2p", k] = send(xsp.at[h, k], x2p.at[h, k], up)
        if k == 1:
            s["xhop", 2].wait_recv()
        if k == 1:
            s["x1m"].wait_recv()
        own = part[h, 2, 2 + k, r_x]
        xsm[h, k, w_a] = (f32(xb[h, 2, k, w_a]) + f32(own[:XH])).astype(BF16)
        xsm[h, k, w_b] = (f32(xb[h, 2, k, w_b]) + f32(own[XH:]) + f32(x1m[h, k])).astype(BF16)
        s["x2m", k] = send(xsm.at[h, k], x2m.at[h, k], down)

    def zsum(h, g):
        s, at = rs[h], pair[g]
        for name in ("plain_p", "plain_m", "sum_p", "sum_m"):
            s[name, g].wait_recv()
        return f32(part[h, 3, at, r_z]) + f32(z2p[h, at]) + f32(z2m[h, at])

    def z_given(h):
        xs[h] = zsum(h, 0).astype(BF16)
        for k in (1, 0):
            rs[h]["xs", k] = send(xs.at[h, k], xr.at[h, k], twin)
            rs[h]["xhop", 3, k] = send(part.at[h, 3, k, r_x], xb.at[h, 3, k], twin)

    def lanes(h):
        return pl.ds(h * WIDE, WIDE)

    def features(h):
        return pl.ds(pl.multiple_of(feat * 256 + h * WIDE, WIDE), WIDE)

    def z_done(h, k):
        s = rs[h]
        value = zsum(h, 2 - k)[0]
        s["xs", k].wait_recv()
        value = (value + f32(xr[h, k])).astype(BF16)
        if k == 1:
            give[r_z, lanes(h)] = value
            s["give_z"] = send(give.at[r_z, lanes(h)], hidden.at[r_z, features(h)], cross)
        else:
            hidden[r_z, features(h)] = value

    def x_done(h, k):
        s = rs[h]
        for name in (("xhop", 3, k), ("x2p", k), ("x2m", k)):
            s[name].wait_recv()
        value = (
            f32(xb[h, 3, k]) + f32(part[h, 3, 2 + k, r_x]) + f32(x2p[h, k]) + f32(x2m[h, k])
        ).astype(BF16)
        if k == 1:
            give[r_x, lanes(h)] = value
            s["give_x"] = send(give.at[r_x, lanes(h)], hidden.at[r_x, features(h)], cross)
        else:
            hidden[r_x, features(h)] = value

    def reduce_start(h):
        collect(h, 0, 1)
        xhop(h, 0)
        for g in range(3):
            hop(h, g)
        collect(h, 1, 4)
        xhop(h, 1)
        plain(h, 0)
        xhop(h, 2)

    def kept(h, k):
        plain(h, 2 - k)
        sums(h, 2 - k)

    def weight_1():
        return [send(gw.at[:, (col + j) % 8], ar1.at[j - 1], others_c[j - 1]) for j in range(1, 8)]

    def weight_2(copies):
        for c in copies:
            c.wait_recv()
        acc = f32(gw[:, col])
        for j in range(7):
            acc = acc + f32(ar1[j])
        for r in range(8):
            ar2s[r] = acc[:, r * 8 : r * 8 + 8, :]
        return [send(ar2s.at[(row + j) % 8], ar2.at[j - 1], others_r[j - 1]) for j in range(1, 8)]

    def weight_3(copies):
        for c in copies:
            c.wait_recv()
        done = ar2s[row]
        for j in range(7):
            done = done + ar2[j]
        ar3[col] = done.reshape(16, 256).astype(BF16)
        return [send(ar3.at[col], ar3.at[col], others_c[j]) for j in range(7)]

    def weight_4(copies):
        for c in copies:
            c.wait_recv()
        ar4[row] = ar3[...]
        return [send(ar3, ar4.at[row], others_r[j]) for j in range(7)]

    zero = jnp.zeros((TILE, WIDE), F32)
    gather_far(1)
    for c in swap:
        c.wait_recv()
    term(lambda: other[0], lambda: other[1], 1 - feat)
    wc = weight_1()
    run = products(0, 0, 2, zero)
    gather_near(1)
    products(0, 2, 4, run)
    gather_last(1)
    reduce_start(0)
    wc = weight_2(wc)
    gather_end(1)
    run = products(1, 0, 2, zero)
    sums(0, 0)
    run = products(1, 2, 4, run)
    x_first(0)
    kept(0, 1)
    kept(0, 0)
    run = products(1, 4, 6, run)
    wc = weight_3(wc)
    z_given(0)
    products(1, 6, 8, run)
    x_second(0, 1)
    x_second(0, 0)
    reduce_start(1)
    wc = weight_4(wc)
    z_done(0, 1)
    z_done(0, 0)
    x_done(0, 1)
    x_done(0, 0)
    sums(1, 0)
    x_first(1)
    kept(1, 1)
    z_given(1)
    x_second(1, 1)
    kept(1, 0)
    x_second(1, 0)
    z_done(1, 1)
    x_done(1, 1)
    z_done(1, 0)
    for c in wc:
        c.wait_recv()
    out = [pltpu.make_async_copy(ar4, pieces_hbm, lsem.at[0])]
    out[0].start()
    x_done(1, 0)
    for at, name in ((r_z, "give_z"), (r_x, "give_x")):
        for h in range(2):
            rs[h][name].wait_recv()
        out.append(pltpu.make_async_copy(hidden.at[at], hidden_hbm.at[at], lsem.at[len(out)]))
        out[-1].start()
    for c in out:
        c.wait()
    for c in started:
        c.wait_send()


def finish_kernel(
    hidden, weight, pieces, grad_in, grad_weight, hidden_v, weight_v, pieces_v, left, right, sems
):
    copies = [pltpu.make_async_copy(hidden, hidden_v, sems.at[0])]
    blocks = [pl.ds(n * 256, 256) for n in range(4)]
    for n, at in enumerate(blocks):
        copies.append(pltpu.make_async_copy(weight.at[at], weight_v.at[at], sems.at[1 + n]))
    copies.append(pltpu.make_async_copy(pieces, pieces_v, sems.at[5]))
    for c in copies:
        c.start()
    copies[0].wait()
    dims = (((1,), (1,)), ((), ()))
    out = []
    for n, at in enumerate(blocks):
        copies[1 + n].wait()
        left[:, at] = lax.dot_general(
            hidden_v[...], weight_v[at], dims, preferred_element_type=F32
        ).astype(BF16)
        out.append(pltpu.make_async_copy(left.at[:, at], grad_in.at[:, at], sems.at[6 + n]))
        out[-1].start()
        if n == 2:
            copies[5].wait()
            for s in range(8):
                for r in range(8):
                    piece = pieces_v[r, s].astype(F32)
                    rows = s * 64 + r * 8
                    for f in range(2):
                        right[rows : rows + 8, f * 256 : f * 256 + 256] = piece[f * 8 : f * 8 + 8]
            out.append(pltpu.make_async_copy(right, grad_weight, sems.at[10]))
            out[-1].start()
    for c in out:
        c.wait()


def finish(hidden, weight, pieces):
    anywhere = pl.BlockSpec(memory_space=pl.ANY)
    return pl.pallas_call(
        finish_kernel,
        in_specs=[anywhere] * 3,
        out_specs=(anywhere, anywhere),
        out_shape=(
            jax.ShapeDtypeStruct((512, 1024), BF16),
            jax.ShapeDtypeStruct((512, 512), F32),
        ),
        scratch_shapes=[
            pltpu.VMEM((512, 512), BF16),
            pltpu.VMEM((1024, 512), BF16),
            pltpu.VMEM((8, 8, 16, 256), BF16),
            pltpu.VMEM((512, 1024), BF16),
            pltpu.VMEM((512, 512), F32),
            pltpu.SemaphoreType.DMA((11,)),
        ],
        compiler_params=pltpu.CompilerParams(vmem_limit_bytes=60 * 2**20),
        name="finish",
    )(hidden, weight, pieces)


COPIES = 2 * 11 + 2 + 2 * 33 + 28


def per_device(grad_out, saved_agg, tile_values, tile_rows, tile_cols, tile_counts, weight):
    anywhere = pl.BlockSpec(memory_space=pl.ANY)
    scratch = [
        ((SLOTS + 1, TILE, TILE), BF16),
        ((64, TILE, WIDE), BF16), ((64, TILE, WIDE), BF16),
        ((STEPS + 1, TILE, WIDE), BF16), ((2, 4, 4, 512, WIDE), BF16),
        ((2, 4, ZH, WIDE), BF16), ((2, 4, ZH, WIDE), BF16),
        ((2, 4, ZR, WIDE), BF16), ((2, 4, ZR, WIDE), BF16),
        ((2, 4, ZH, WIDE), BF16), ((2, 4, ZH, WIDE), BF16),
        ((2, 2, ZR, WIDE), BF16), ((2, 2, ZR, WIDE), BF16),
        ((2, 4, 2, XR, WIDE), BF16),
        ((2, 2, XH, WIDE), BF16), ((2, 2, XH, WIDE), BF16),
        ((2, 2, XR, WIDE), BF16), ((2, 2, XR, WIDE), BF16),
        ((2, 2, XR, WIDE), BF16), ((2, 2, XR, WIDE), BF16), ((2, 2, XR, WIDE), BF16),
        ((512, 256), BF16), ((512, 512), BF16), ((8, TILE, 256), BF16), ((1024, 512), BF16), ((2, 8, TILE, WIDE), BF16),
        ((2, 8, 64, 256), BF16),
        ((7, 2, 64, 256), BF16), ((8, 2, 8, 256), F32), ((7, 2, 8, 256), F32),
        ((8, 16, 256), BF16), ((8, 8, 16, 256), BF16),
        ((1, SLOTS), I32), ((1, SLOTS), I32), ((1, 1), I32), ((1, PLACES), I32), ((1, TILE), I32),
    ]
    hidden, pieces = pl.pallas_call(
        fused_kernel,
        out_shape=(
            jax.ShapeDtypeStruct((512, 512), BF16),
            jax.ShapeDtypeStruct((8, 8, 16, 256), BF16),
        ),
        in_specs=[anywhere] * 6,
        out_specs=(anywhere, anywhere),
        scratch_shapes=[pltpu.VMEM(s, t) for s, t in scratch]
        + [pltpu.SMEM((1, PLACES), I32), pltpu.SMEM((1, TILE), I32)]
        + [
            pltpu.SemaphoreType.DMA((COPIES,)),
            pltpu.SemaphoreType.DMA((COPIES,)),
            pltpu.SemaphoreType.DMA((25,)),
        ],
        compiler_params=pltpu.CompilerParams(
            collective_id=0, has_side_effects=True, vmem_limit_bytes=56 * 2**20
        ),
        name="fused",
    )(
        tile_rows[0], tile_cols[0], tile_counts,
        grad_out.reshape(8, TILE, 256), saved_agg, tile_values[0, 0],
    )
    return finish(hidden, weight, pieces)


def solution(mesh):
    in_specs = (
        P(("row", "col"), "feat"),
        P(("row", "col"), "feat"),
        P("row", "col", None, None, None),
        P("row", "col", None),
        P("row", "col", None),
        P("row", "col"),
        P(),
    )
    out_specs = (P(("row", "col", "feat"), None), P("feat", None))
    return jax.shard_map(
        per_device, mesh=mesh, in_specs=in_specs, out_specs=out_specs, check_vma=False
    )
```

```python
import jax
import jax.numpy as jnp
from jax import lax
from jax.experimental import pallas as pl
from jax.experimental.pallas import tpu as pltpu
from jax.sharding import PartitionSpec as P

MESH = pl.DeviceIdType.MESH
F32 = jnp.float32
BF16 = jnp.bfloat16
I32 = jnp.int32

TILE = 128
ROW_TILES = 64
SLOTS = 640
STEPS = 352
PLACES = 768
UNROLL = (88, 44)
CHUNKS = 16
WIDE = 128

XR = 224
ZR = 288
XH, ZH = XR // 2, ZR // 2
GIVE, KEEP = pl.ds(0, 2), pl.ds(2, 2)


def fused_kernel(
    rows_hbm, cols_hbm, count_hbm, x_hbm, saved_hbm, tiles_hbm,
    hidden_hbm, pieces_hbm,
    held, panel0, panel1, slots, part,
    z1p, z1m, z2p, z2m, zsp, zsm, xs, xr, xb, x1p, x1m, x2p, x2m, xw, xsp, xsm,
    give, hidden, x_v, saved, other, gw, ar1, ar2s, ar2, ar3, ar4,
    rows_ref, cols_ref, count_ref, table_v, last_v, table, last,
    ssem, rsem, lsem,
):
    row, col, feat = (lax.axis_index(a) for a in ("row", "col", "feat"))
    y, core, x, z = row // 2, row % 2, col // 4, col % 4
    panels = (panel0, panel1)
    y_up = (((y + 1) % 4) * 2 + core, col, feat)
    y_down = (((y + 3) % 4) * 2 + core, col, feat)
    chip_mate = (y * 2 + 1 - core, col, feat)
    mate = (row, col, 1 - feat)
    up, down = (row, x * 4 + (z + 1) % 4, feat), (row, x * 4 + (z + 3) % 4, feat)
    twin = (row, (1 - x) * 4 + z, feat)
    cross = (row, (1 - x) * 4 + z, 1 - feat)
    others_r = [((row + j) % 8, col, feat) for j in range(1, 8)]
    others_c = [(row, (col + j) % 8, feat) for j in range(1, 8)]
    started = []

    def send(src, dst, to):
        i = len(started)
        copy = pltpu.make_async_remote_copy(
            src_ref=src, dst_ref=dst, send_sem=ssem.at[i], recv_sem=rsem.at[i],
            device_id=to, device_id_type=MESH,
        )
        copy.start()
        started.append(copy)
        return copy

    def f32(value):
        return value.astype(F32)

    barrier = pltpu.get_barrier_semaphore()
    friends = others_r + others_c + [mate, cross]
    for d in friends:
        pl.semaphore_signal(barrier, inc=1, device_id=d, device_id_type=MESH)

    local = [
        pltpu.make_async_copy(x_hbm, x_v, lsem.at[0]),
        pltpu.make_async_copy(saved_hbm, saved, lsem.at[1]),
    ]
    tables = [
        pltpu.make_async_copy(rows_hbm, rows_ref, lsem.at[22]),
        pltpu.make_async_copy(cols_hbm, cols_ref, lsem.at[23]),
        pltpu.make_async_copy(count_hbm, count_ref, lsem.at[24]),
    ]
    each = SLOTS // CHUNKS
    for n in range(CHUNKS):
        at = pl.ds(n * each, each)
        local.append(pltpu.make_async_copy(tiles_hbm.at[at], held.at[at], lsem.at[2 + n]))
    for c in local[:1] + tables + local[1:]:
        c.start()
    pl.semaphore_wait(barrier, len(friends))

    r_down, r_up, r_far = (((y + k) % 4) * 2 + core for k in (3, 1, 2))

    def shard(h, r, half=None):
        at = pl.ds(r * 8, 8) if half is None else pl.ds(r * 8 + half * 4, 4)
        return panels[h].at[at]

    def pass_on(h, r, to, half=None):
        return send(shard(h, r, half), shard(h, r, half), to)

    ag = ({}, {})

    def gather_first(h):
        a = ag[h]
        a["up0"], a["down1"] = pass_on(h, row, y_up, 0), pass_on(h, row, y_down, 1)
        a["up1"], a["down0"] = pass_on(h, row, y_up, 1), pass_on(h, row, y_down, 0)
        a["core"] = pass_on(h, row, chip_mate)

    def gather_far(h):
        a = ag[h]
        a["up0"].wait_recv()
        a["far0"] = pass_on(h, r_down, y_up, 0)
        a["down1"].wait_recv()
        a["far1"] = pass_on(h, r_up, y_down, 1)

    def gather_near(h):
        a = ag[h]
        a["up1"].wait_recv()
        a["core_d"] = pass_on(h, r_down, chip_mate)
        a["down0"].wait_recv()
        a["core_u"] = pass_on(h, r_up, chip_mate)

    def gather_last(h):
        a = ag[h]
        a["far0"].wait_recv()
        a["core_f0"] = pass_on(h, r_far, chip_mate, 0)
        a["far1"].wait_recv()
        a["core_f1"] = pass_on(h, r_far, chip_mate, 1)

    def gather_end(h):
        for name in ("core", "core_d", "core_u", "core_f0", "core_f1"):
            ag[h][name].wait_recv()

    mine = pl.ds(row * 8, 8)
    local[0].wait()
    panel0[mine] = x_v[:, :, :WIDE]
    gather_first(0)
    panel1[mine] = x_v[:, :, WIDE:]
    swap = [send(shard(h, row), other.at[h], mate) for h in range(2)]

    def iota(shape, axis):
        return lax.broadcasted_iota(I32, shape, axis)

    def total(mask, value, axis):
        return jnp.sum(jnp.where(mask, value, 0), axis=axis, keepdims=True)

    for c in tables:
        c.wait()
    count = count_ref[...]
    slot_r = iota((1, SLOTS), 1)
    slot_c = iota((SLOTS, 1), 0)
    eye = iota((SLOTS, SLOTS), 0) == iota((SLOTS, SLOTS), 1)
    rows_r = jnp.where(slot_r < count, rows_ref[...], ROW_TILES)
    rows_c = total(eye, rows_r, 1)
    cols_c = total(eye, cols_ref[...], 1)
    tile_r, tile_c = iota((1, TILE), 1), iota((TILE, 1), 0)
    n_c = total(rows_r == tile_c, 1, 1)
    n_r = total(rows_c == tile_r, 1, 0)
    n_c = jnp.where(tile_c < ROW_TILES, (n_c + 1) >> 1, 0)
    n_r = jnp.where(tile_r < ROW_TILES, (n_r + 1) >> 1, 0)
    end_r = total(tile_c <= tile_r, n_c, 0)
    start_r = end_r - n_r
    before = total((rows_r == rows_c) & (slot_r < slot_c), 1, 1)
    first = total(rows_c == tile_r, start_r, 1)
    place = jnp.where(rows_c < ROW_TILES, first * 2 + before, PLACES)
    at_r = iota((1, PLACES), 1)
    empty = SLOTS * 64
    word = total(place == at_r, slot_c * 64 + cols_c - empty, 0) + empty
    start_c = total(tile_c == tile_r, start_r, 1)
    opens = total((start_c * 2 == at_r) & (n_c > 0), 1, 0)
    table_v[...] = word + opens * 65536
    last_v[...] = jnp.where(n_r > 0, end_r - 1, STEPS)
    fill = [
        pltpu.make_async_copy(table_v, table, lsem.at[20]),
        pltpu.make_async_copy(last_v, last, lsem.at[21]),
    ]
    for c in fill:
        c.start()

    gather_far(0)
    gather_first(1)

    def term(low, high, slot):
        def columns(n, _):
            at = pl.ds(pl.multiple_of(n * 128, 128), 128)
            source = jnp.concatenate([low().reshape(8 * TILE, WIDE), high().reshape(8 * TILE, WIDE)], axis=1)
            value = lax.dot_general(
                saved[:, at], source, (((0,), (0,)), ((), ())), preferred_element_type=F32
            )
            gw[slot, pl.ds(n * 2, 2)] = value.astype(BF16).reshape(2, 64, 256)
            return 0

        lax.fori_loop(0, 4, columns, 0)

    local[1].wait()
    term(lambda: panel0[mine], lambda: panel1[mine], feat)
    gather_near(0)
    held[SLOTS] = jnp.zeros((TILE, TILE), BF16)
    slots[STEPS] = jnp.zeros((TILE, WIDE), BF16)
    for c in local[2:] + fill:
        c.wait()
    gather_last(0)
    gather_end(0)

    def products(h, lo, hi, sums):
        panel = panels[h]

        def group(g, sums):
            for u in range(UNROLL[h]):
                p = g * UNROLL[h] + u
                w = [table[0, 2 * p + i] for i in range(2)]
                left = jnp.concatenate([held[(a >> 6) & 1023] for a in w], axis=1)
                right = jnp.concatenate([panel[a & 63] for a in w], axis=0)
                fresh = jnp.dot(left, right, preferred_element_type=F32)
                sums = fresh + jnp.where((w[0] >> 16) > 0, 0.0, sums)
                slots[p] = sums.astype(BF16)
            return sums

        return lax.fori_loop(lo, hi, group, sums)

    quarters = ((1 - x, feat), (x, 1 - feat), (x, feat), (1 - x, 1 - feat))
    offsets = (2, 1, 3, 0)

    def collect(h, first, end):
        for o in range(first, end):
            for q in range(4):
                xx, half = quarters[q]
                base = (xx * 4 + (z + offsets[o]) % 4) * 8 + half * 4
                for t in range(4):
                    part[h, o, q, t * TILE : (t + 1) * TILE] = slots[last[0, base + t]]

    r_x, r_z = pl.ds(0, XR), pl.ds(XR, ZR)
    r_a, r_b = pl.ds(XR, ZH), pl.ds(XR + ZH, ZH)
    v_a, v_b = pl.ds(0, ZH), pl.ds(ZH, ZH)
    w_a, w_b = pl.ds(0, XH), pl.ds(XH, XH)
    rs = ({}, {})
    pair = (GIVE, pl.ds(3, 1), pl.ds(2, 1))

    def xhop(h, o):
        rs[h]["xhop", o] = send(part.at[h, o, GIVE, r_x], xb.at[h, o], twin)

    def hop(h, g):
        s, at = rs[h], pair[g]
        s["hop_p", g] = send(part.at[h, 0, at, r_a], z1p.at[h, at], up)
        s["hop_m", g] = send(part.at[h, 0, at, r_b], z1m.at[h, at], down)

    def plain(h, g):
        s, at = rs[h], pair[g]
        s["plain_p", g] = send(part.at[h, 1, at, r_b], z2p.at[h, at, v_b], up)
        s["plain_m", g] = send(part.at[h, 2, at, r_a], z2m.at[h, at, v_a], down)

    def sums(h, g):
        s, at = rs[h], pair[g]
        s["hop_p", g].wait_recv()
        zsp[h, at] = (f32(z1p[h, at]) + f32(part[h, 1, at, r_a])).astype(BF16)
        s["sum_p", g] = send(zsp.at[h, at], z2p.at[h, at, v_a], up)
        s["hop_m", g].wait_recv()
        zsm[h, at] = (f32(z1m[h, at]) + f32(part[h, 2, at, r_b])).astype(BF16)
        s["sum_m", g] = send(zsm.at[h, at], z2m.at[h, at, v_b], down)

    def x_first(h):
        s = rs[h]
        s["xhop", 0].wait_recv()
        xw[h] = (f32(xb[h, 0]) + f32(part[h, 0, KEEP, r_x])).astype(BF16)
        s["x1p"] = send(xw.at[h, :, w_a], x1p.at[h], up)
        s["x1m"] = send(xw.at[h, :, w_b], x1m.at[h], down)

    def x_second(h, k):
        s = rs[h]
        if k == 1:
            s["xhop", 1].wait_recv()
        if k == 1:
            s["x1p"].wait_recv()
        own = part[h, 1, 2 + k, r_x]
        xsp[h, k, w_a] = (f32(xb[h, 1, k, w_a]) + f32(own[:XH]) + f32(x1p[h, k])).astype(BF16)
        xsp[h, k, w_b] = (f32(xb[h, 1, k, w_b]) + f32(own[XH:])).astype(BF16)
        s["x2p", k] = send(xsp.at[h, k], x2p.at[h, k], up)
        if k == 1:
            s["xhop", 2].wait_recv()
        if k == 1:
            s["x1m"].wait_recv()
        own = part[h, 2, 2 + k, r_x]
        xsm[h, k, w_a] = (f32(xb[h, 2, k, w_a]) + f32(own[:XH])).astype(BF16)
        xsm[h, k, w_b] = (f32(xb[h, 2, k, w_b]) + f32(own[XH:]) + f32(x1m[h, k])).astype(BF16)
        s["x2m", k] = send(xsm.at[h, k], x2m.at[h, k], down)

    def zsum(h, g):
        s, at = rs[h], pair[g]
        for name in ("plain_p", "plain_m", "sum_p", "sum_m"):
            s[name, g].wait_recv()
        return f32(part[h, 3, at, r_z]) + f32(z2p[h, at]) + f32(z2m[h, at])

    def z_given(h):
        xs[h] = zsum(h, 0).astype(BF16)
        for k in (1, 0):
            rs[h]["xs", k] = send(xs.at[h, k], xr.at[h, k], twin)
            rs[h]["xhop", 3, k] = send(part.at[h, 3, k, r_x], xb.at[h, 3, k], twin)

    def lanes(h):
        return pl.ds(h * WIDE, WIDE)

    def features(h):
        return pl.ds(pl.multiple_of(feat * 256 + h * WIDE, WIDE), WIDE)

    def z_done(h, k):
        s = rs[h]
        value = zsum(h, 2 - k)[0]
        s["xs", k].wait_recv()
        value = (value + f32(xr[h, k])).astype(BF16)
        if k == 1:
            give[r_z, lanes(h)] = value
            s["give_z"] = send(give.at[r_z, lanes(h)], hidden.at[r_z, features(h)], cross)
        else:
            hidden[r_z, features(h)] = value

    def x_done(h, k):
        s = rs[h]
        for name in (("xhop", 3, k), ("x2p", k), ("x2m", k)):
            s[name].wait_recv()
        value = (
            f32(xb[h, 3, k]) + f32(part[h, 3, 2 + k, r_x]) + f32(x2p[h, k]) + f32(x2m[h, k])
        ).astype(BF16)
        if k == 1:
            give[r_x, lanes(h)] = value
            s["give_x"] = send(give.at[r_x, lanes(h)], hidden.at[r_x, features(h)], cross)
        else:
            hidden[r_x, features(h)] = value

    def reduce_start(h):
        collect(h, 0, 1)
        xhop(h, 0)
        for g in range(3):
            hop(h, g)
        collect(h, 1, 4)
        xhop(h, 1)
        plain(h, 0)
        xhop(h, 2)

    def kept(h, k):
        plain(h, 2 - k)
        sums(h, 2 - k)

    def weight_1():
        return [send(gw.at[:, (col + j) % 8], ar1.at[j - 1], others_c[j - 1]) for j in range(1, 8)]

    def weight_2(copies):
        for c in copies:
            c.wait_recv()
        acc = f32(gw[:, col])
        for j in range(7):
            acc = acc + f32(ar1[j])
        for r in range(8):
            ar2s[r] = acc[:, r * 8 : r * 8 + 8, :]
        return [send(ar2s.at[(row + j) % 8], ar2.at[j - 1], others_r[j - 1]) for j in range(1, 8)]

    def weight_3(copies):
        for c in copies:
            c.wait_recv()
        done = ar2s[row]
        for j in range(7):
            done = done + ar2[j]
        ar3[col] = done.reshape(16, 256).astype(BF16)
        return [send(ar3.at[col], ar3.at[col], others_c[j]) for j in range(7)]

    def weight_4(copies):
        for c in copies:
            c.wait_recv()
        ar4[row] = ar3[...]
        return [send(ar3, ar4.at[row], others_r[j]) for j in range(7)]

    zero = jnp.zeros((TILE, WIDE), F32)
    gather_far(1)
    for c in swap:
        c.wait_recv()
    term(lambda: other[0], lambda: other[1], 1 - feat)
    wc = weight_1()
    run = products(0, 0, 2, zero)
    gather_near(1)
    products(0, 2, 4, run)
    gather_last(1)
    reduce_start(0)
    wc = weight_2(wc)
    gather_end(1)
    run = products(1, 0, 2, zero)
    sums(0, 0)
    run = products(1, 2, 4, run)
    x_first(0)
    kept(0, 1)
    kept(0, 0)
    run = products(1, 4, 6, run)
    wc = weight_3(wc)
    z_given(0)
    products(1, 6, 8, run)
    x_second(0, 1)
    x_second(0, 0)
    reduce_start(1)
    wc = weight_4(wc)
    z_done(0, 1)
    z_done(0, 0)
    x_done(0, 1)
    x_done(0, 0)
    sums(1, 0)
    x_first(1)
    kept(1, 1)
    z_given(1)
    x_second(1, 1)
    kept(1, 0)
    x_second(1, 0)
    z_done(1, 1)
    x_done(1, 1)
    z_done(1, 0)
    for c in wc:
        c.wait_recv()
    out = [pltpu.make_async_copy(ar4, pieces_hbm, lsem.at[0])]
    out[0].start()
    x_done(1, 0)
    for at, name in ((r_z, "give_z"), (r_x, "give_x")):
        for h in range(2):
            rs[h][name].wait_recv()
        out.append(pltpu.make_async_copy(hidden.at[at], hidden_hbm.at[at], lsem.at[len(out)]))
        out[-1].start()
    for c in out:
        c.wait()
    for c in started:
        c.wait_send()


def finish_kernel(
    hidden, weight, pieces, grad_in, grad_weight, hidden_v, weight_v, pieces_v, left, right, sems
):
    copies = [pltpu.make_async_copy(hidden, hidden_v, sems.at[0])]
    blocks = [pl.ds(n * 256, 256) for n in range(4)]
    for n, at in enumerate(blocks):
        copies.append(pltpu.make_async_copy(weight.at[at], weight_v.at[at], sems.at[1 + n]))
    copies.append(pltpu.make_async_copy(pieces, pieces_v, sems.at[5]))
    for i in (0, 1, 5, 2, 3, 4):
        copies[i].start()
    copies[0].wait()
    dims = (((1,), (1,)), ((), ()))
    out = []
    for n, at in enumerate(blocks):
        copies[1 + n].wait()
        left[:, at] = lax.dot_general(
            hidden_v[...], weight_v[at], dims, preferred_element_type=F32
        ).astype(BF16)
        out.append(pltpu.make_async_copy(left.at[:, at], grad_in.at[:, at], sems.at[6 + n]))
        out[-1].start()
        if n == 0:
            copies[5].wait()
            for s in range(8):
                for r in range(8):
                    piece = pieces_v[r, s].astype(F32)
                    rows = s * 64 + r * 8
                    for f in range(2):
                        right[rows : rows + 8, f * 256 : f * 256 + 256] = piece[f * 8 : f * 8 + 8]
            out.append(pltpu.make_async_copy(right, grad_weight, sems.at[10]))
            out[-1].start()
    for c in out:
        c.wait()


def finish(hidden, weight, pieces):
    anywhere = pl.BlockSpec(memory_space=pl.ANY)
    return pl.pallas_call(
        finish_kernel,
        in_specs=[anywhere] * 3,
        out_specs=(anywhere, anywhere),
        out_shape=(
            jax.ShapeDtypeStruct((512, 1024), BF16),
            jax.ShapeDtypeStruct((512, 512), F32),
        ),
        scratch_shapes=[
            pltpu.VMEM((512, 512), BF16),
            pltpu.VMEM((1024, 512), BF16),
            pltpu.VMEM((8, 8, 16, 256), BF16),
            pltpu.VMEM((512, 1024), BF16),
            pltpu.VMEM((512, 512), F32),
            pltpu.SemaphoreType.DMA((11,)),
        ],
        compiler_params=pltpu.CompilerParams(vmem_limit_bytes=60 * 2**20),
        name="finish",
    )(hidden, weight, pieces)


COPIES = 2 * 11 + 2 + 2 * 33 + 28


def per_device(grad_out, saved_agg, tile_values, tile_rows, tile_cols, tile_counts, weight):
    anywhere = pl.BlockSpec(memory_space=pl.ANY)
    scratch = [
        ((SLOTS + 1, TILE, TILE), BF16),
        ((64, TILE, WIDE), BF16), ((64, TILE, WIDE), BF16),
        ((STEPS + 1, TILE, WIDE), BF16), ((2, 4, 4, 512, WIDE), BF16),
        ((2, 4, ZH, WIDE), BF16), ((2, 4, ZH, WIDE), BF16),
        ((2, 4, ZR, WIDE), BF16), ((2, 4, ZR, WIDE), BF16),
        ((2, 4, ZH, WIDE), BF16), ((2, 4, ZH, WIDE), BF16),
        ((2, 2, ZR, WIDE), BF16), ((2, 2, ZR, WIDE), BF16),
        ((2, 4, 2, XR, WIDE), BF16),
        ((2, 2, XH, WIDE), BF16), ((2, 2, XH, WIDE), BF16),
        ((2, 2, XR, WIDE), BF16), ((2, 2, XR, WIDE), BF16),
        ((2, 2, XR, WIDE), BF16), ((2, 2, XR, WIDE), BF16), ((2, 2, XR, WIDE), BF16),
        ((512, 256), BF16), ((512, 512), BF16), ((8, TILE, 256), BF16), ((1024, 512), BF16), ((2, 8, TILE, WIDE), BF16),
        ((2, 8, 64, 256), BF16),
        ((7, 2, 64, 256), BF16), ((8, 2, 8, 256), F32), ((7, 2, 8, 256), F32),
        ((8, 16, 256), BF16), ((8, 8, 16, 256), BF16),
        ((1, SLOTS), I32), ((1, SLOTS), I32), ((1, 1), I32), ((1, PLACES), I32), ((1, TILE), I32),
    ]
    hidden, pieces = pl.pallas_call(
        fused_kernel,
        out_shape=(
            jax.ShapeDtypeStruct((512, 512), BF16),
            jax.ShapeDtypeStruct((8, 8, 16, 256), BF16),
        ),
        in_specs=[anywhere] * 6,
        out_specs=(anywhere, anywhere),
        scratch_shapes=[pltpu.VMEM(s, t) for s, t in scratch]
        + [pltpu.SMEM((1, PLACES), I32), pltpu.SMEM((1, TILE), I32)]
        + [
            pltpu.SemaphoreType.DMA((COPIES,)),
            pltpu.SemaphoreType.DMA((COPIES,)),
            pltpu.SemaphoreType.DMA((25,)),
        ],
        compiler_params=pltpu.CompilerParams(
            collective_id=0, has_side_effects=True, vmem_limit_bytes=56 * 2**20
        ),
        name="fused",
    )(
        tile_rows[0], tile_cols[0], tile_counts,
        grad_out.reshape(8, TILE, 256), saved_agg, tile_values[0, 0],
    )
    return finish(hidden, weight, pieces)


def solution(mesh):
    in_specs = (
        P(("row", "col"), "feat"),
        P(("row", "col"), "feat"),
        P("row", "col", None, None, None),
        P("row", "col", None),
        P("row", "col", None),
        P("row", "col"),
        P(),
    )
    out_specs = (P(("row", "col", "feat"), None), P("feat", None))
    return jax.shard_map(
        per_device, mesh=mesh, in_specs=in_specs, out_specs=out_specs, check_vma=False
    )
```

```python
import jax
import jax.numpy as jnp
from jax import lax
from jax.experimental import pallas as pl
from jax.experimental.pallas import tpu as pltpu
from jax.sharding import PartitionSpec as P

MESH = pl.DeviceIdType.MESH
F32 = jnp.float32
BF16 = jnp.bfloat16
I32 = jnp.int32

TILE = 128
ROW_TILES = 64
SLOTS = 640
STEPS = 352
PLACES = 768
UNROLL = (88, 44)
CHUNKS = 16
WIDE = 128

XR = 224
ZR = 288
XH, ZH = XR // 2, ZR // 2
GIVE, KEEP = pl.ds(0, 2), pl.ds(2, 2)


def fused_kernel(
    rows_hbm, cols_hbm, count_hbm, x_hbm, saved_hbm, tiles_hbm,
    hidden_hbm, pieces_hbm,
    held, panel0, panel1, slots, part,
    z1p, z1m, z2p, z2m, zsp, zsm, xs, xr, xb, x1p, x1m, x2p, x2m, xw, xsp, xsm,
    give, hidden, x_v, saved, other, gw, ar1, ar2s, ar2, ar3, ar4,
    rows_ref, cols_ref, count_ref, table_v, last_v, table, last,
    ssem, rsem, lsem,
):
    row, col, feat = (lax.axis_index(a) for a in ("row", "col", "feat"))
    y, core, x, z = row // 2, row % 2, col // 4, col % 4
    panels = (panel0, panel1)
    y_up = (((y + 1) % 4) * 2 + core, col, feat)
    y_down = (((y + 3) % 4) * 2 + core, col, feat)
    chip_mate = (y * 2 + 1 - core, col, feat)
    mate = (row, col, 1 - feat)
    up, down = (row, x * 4 + (z + 1) % 4, feat), (row, x * 4 + (z + 3) % 4, feat)
    twin = (row, (1 - x) * 4 + z, feat)
    cross = (row, (1 - x) * 4 + z, 1 - feat)
    others_r = [((row + j) % 8, col, feat) for j in range(1, 8)]
    others_c = [(row, (col + j) % 8, feat) for j in range(1, 8)]
    started = []

    def send(src, dst, to):
        i = len(started)
        copy = pltpu.make_async_remote_copy(
            src_ref=src, dst_ref=dst, send_sem=ssem.at[i], recv_sem=rsem.at[i],
            device_id=to, device_id_type=MESH,
        )
        copy.start()
        started.append(copy)
        return copy

    def f32(value):
        return value.astype(F32)

    barrier = pltpu.get_barrier_semaphore()
    friends = others_r + others_c + [mate, cross]
    for d in friends:
        pl.semaphore_signal(barrier, inc=1, device_id=d, device_id_type=MESH)

    local = [
        pltpu.make_async_copy(x_hbm, x_v, lsem.at[0]),
        pltpu.make_async_copy(saved_hbm, saved, lsem.at[1]),
    ]
    tables = [
        pltpu.make_async_copy(rows_hbm, rows_ref, lsem.at[22]),
        pltpu.make_async_copy(cols_hbm, cols_ref, lsem.at[23]),
        pltpu.make_async_copy(count_hbm, count_ref, lsem.at[24]),
    ]
    each = SLOTS // CHUNKS
    for n in range(CHUNKS):
        at = pl.ds(n * each, each)
        local.append(pltpu.make_async_copy(tiles_hbm.at[at], held.at[at], lsem.at[2 + n]))
    for c in local[:1] + tables + local[1:]:
        c.start()
    pl.semaphore_wait(barrier, len(friends))

    r_down, r_up, r_far = (((y + k) % 4) * 2 + core for k in (3, 1, 2))

    def shard(h, r, half=None):
        at = pl.ds(r * 8, 8) if half is None else pl.ds(r * 8 + half * 4, 4)
        return panels[h].at[at]

    def pass_on(h, r, to, half=None):
        return send(shard(h, r, half), shard(h, r, half), to)

    ag = ({}, {})

    def gather_first(h):
        a = ag[h]
        a["up0"], a["down1"] = pass_on(h, row, y_up, 0), pass_on(h, row, y_down, 1)
        a["up1"], a["down0"] = pass_on(h, row, y_up, 1), pass_on(h, row, y_down, 0)
        a["core"] = pass_on(h, row, chip_mate)

    def gather_far(h):
        a = ag[h]
        a["up0"].wait_recv()
        a["far0"] = pass_on(h, r_down, y_up, 0)
        a["down1"].wait_recv()
        a["far1"] = pass_on(h, r_up, y_down, 1)

    def gather_near(h):
        a = ag[h]
        a["up1"].wait_recv()
        a["core_d"] = pass_on(h, r_down, chip_mate)
        a["down0"].wait_recv()
        a["core_u"] = pass_on(h, r_up, chip_mate)

    def gather_last(h):
        a = ag[h]
        a["far0"].wait_recv()
        a["core_f0"] = pass_on(h, r_far, chip_mate, 0)
        a["far1"].wait_recv()
        a["core_f1"] = pass_on(h, r_far, chip_mate, 1)

    def gather_end(h):
        for name in ("core", "core_d", "core_u", "core_f0", "core_f1"):
            ag[h][name].wait_recv()

    mine = pl.ds(row * 8, 8)
    local[0].wait()
    panel0[mine] = x_v[:, :, :WIDE]
    gather_first(0)
    panel1[mine] = x_v[:, :, WIDE:]
    swap = [send(shard(h, row), other.at[h], mate) for h in range(2)]

    def iota(shape, axis):
        return lax.broadcasted_iota(I32, shape, axis)

    def total(mask, value, axis):
        return jnp.sum(jnp.where(mask, value, 0), axis=axis, keepdims=True)

    for c in tables:
        c.wait()
    count = count_ref[...]
    slot_r = iota((1, SLOTS), 1)
    slot_c = iota((SLOTS, 1), 0)
    eye = iota((SLOTS, SLOTS), 0) == iota((SLOTS, SLOTS), 1)
    rows_r = jnp.where(slot_r < count, rows_ref[...], ROW_TILES)
    rows_c = total(eye, rows_r, 1)
    cols_c = total(eye, cols_ref[...], 1)
    tile_r, tile_c = iota((1, TILE), 1), iota((TILE, 1), 0)
    n_c = total(rows_r == tile_c, 1, 1)
    n_r = total(rows_c == tile_r, 1, 0)
    n_c = jnp.where(tile_c < ROW_TILES, (n_c + 1) >> 1, 0)
    n_r = jnp.where(tile_r < ROW_TILES, (n_r + 1) >> 1, 0)
    end_r = total(tile_c <= tile_r, n_c, 0)
    start_r = end_r - n_r
    before = total((rows_r == rows_c) & (slot_r < slot_c), 1, 1)
    first = total(rows_c == tile_r, start_r, 1)
    place = jnp.where(rows_c < ROW_TILES, first * 2 + before, PLACES)
    at_r = iota((1, PLACES), 1)
    empty = SLOTS * 64
    word = total(place == at_r, slot_c * 64 + cols_c - empty, 0) + empty
    start_c = total(tile_c == tile_r, start_r, 1)
    opens = total((start_c * 2 == at_r) & (n_c > 0), 1, 0)
    table_v[...] = word + opens * 65536
    last_v[...] = jnp.where(n_r > 0, end_r - 1, STEPS)
    fill = [
        pltpu.make_async_copy(table_v, table, lsem.at[20]),
        pltpu.make_async_copy(last_v, last, lsem.at[21]),
    ]
    for c in fill:
        c.start()

    gather_far(0)
    gather_first(1)

    def term(low, high, slot):
        def columns(n, _):
            at = pl.ds(pl.multiple_of(n * 128, 128), 128)
            source = jnp.concatenate([low().reshape(8 * TILE, WIDE), high().reshape(8 * TILE, WIDE)], axis=1)
            value = lax.dot_general(
                saved[:, at], source, (((0,), (0,)), ((), ())), preferred_element_type=F32
            )
            gw[slot, pl.ds(n * 2, 2)] = value.astype(BF16).reshape(2, 64, 256)
            return 0

        lax.fori_loop(0, 4, columns, 0)

    local[1].wait()
    term(lambda: panel0[mine], lambda: panel1[mine], feat)
    gather_near(0)
    held[SLOTS] = jnp.zeros((TILE, TILE), BF16)
    slots[STEPS] = jnp.zeros((TILE, WIDE), BF16)
    for c in local[2:] + fill:
        c.wait()
    gather_last(0)
    gather_end(0)

    def products(h, lo, hi, sums):
        panel = panels[h]

        def group(g, sums):
            for u in range(UNROLL[h]):
                p = g * UNROLL[h] + u
                w = [table[0, 2 * p + i] for i in range(2)]
                left = jnp.concatenate([held[(a >> 6) & 1023] for a in w], axis=1)
                right = jnp.concatenate([panel[a & 63] for a in w], axis=0)
                fresh = jnp.dot(left, right, preferred_element_type=F32)
                sums = fresh + jnp.where((w[0] >> 16) > 0, 0.0, sums)
                slots[p] = sums.astype(BF16)
            return sums

        return lax.fori_loop(lo, hi, group, sums)

    quarters = ((1 - x, feat), (x, 1 - feat), (x, feat), (1 - x, 1 - feat))
    offsets = (2, 1, 3, 0)

    def collect(h, first, end):
        for o in range(first, end):
            for q in range(4):
                xx, half = quarters[q]
                base = (xx * 4 + (z + offsets[o]) % 4) * 8 + half * 4
                for t in range(4):
                    part[h, o, q, t * TILE : (t + 1) * TILE] = slots[last[0, base + t]]

    r_x, r_z = pl.ds(0, XR), pl.ds(XR, ZR)
    r_a, r_b = pl.ds(XR, ZH), pl.ds(XR + ZH, ZH)
    v_a, v_b = pl.ds(0, ZH), pl.ds(ZH, ZH)
    w_a, w_b = pl.ds(0, XH), pl.ds(XH, XH)
    rs = ({}, {})
    pair = (GIVE, pl.ds(3, 1), pl.ds(2, 1))

    def xhop(h, o):
        rs[h]["xhop", o] = send(part.at[h, o, GIVE, r_x], xb.at[h, o], twin)

    def hop(h, g):
        s, at = rs[h], pair[g]
        s["hop_p", g] = send(part.at[h, 0, at, r_a], z1p.at[h, at], up)
        s["hop_m", g] = send(part.at[h, 0, at, r_b], z1m.at[h, at], down)

    def plain(h, g):
        s, at = rs[h], pair[g]
        s["plain_p", g] = send(part.at[h, 1, at, r_b], z2p.at[h, at, v_b], up)
        s["plain_m", g] = send(part.at[h, 2, at, r_a], z2m.at[h, at, v_a], down)

    def sums(h, g):
        s, at = rs[h], pair[g]
        s["hop_p", g].wait_recv()
        zsp[h, at] = (f32(z1p[h, at]) + f32(part[h, 1, at, r_a])).astype(BF16)
        s["sum_p", g] = send(zsp.at[h, at], z2p.at[h, at, v_a], up)
        s["hop_m", g].wait_recv()
        zsm[h, at] = (f32(z1m[h, at]) + f32(part[h, 2, at, r_b])).astype(BF16)
        s["sum_m", g] = send(zsm.at[h, at], z2m.at[h, at, v_b], down)

    def x_first(h):
        s = rs[h]
        s["xhop", 0].wait_recv()
        xw[h] = (f32(xb[h, 0]) + f32(part[h, 0, KEEP, r_x])).astype(BF16)
        s["x1p"] = send(xw.at[h, :, w_a], x1p.at[h], up)
        s["x1m"] = send(xw.at[h, :, w_b], x1m.at[h], down)

    def x_second(h, k):
        s = rs[h]
        if k == 1:
            s["xhop", 1].wait_recv()
        if k == 1:
            s["x1p"].wait_recv()
        own = part[h, 1, 2 + k, r_x]
        xsp[h, k, w_a] = (f32(xb[h, 1, k, w_a]) + f32(own[:XH]) + f32(x1p[h, k])).astype(BF16)
        xsp[h, k, w_b] = (f32(xb[h, 1, k, w_b]) + f32(own[XH:])).astype(BF16)
        s["x2p", k] = send(xsp.at[h, k], x2p.at[h, k], up)
        if k == 1:
            s["xhop", 2].wait_recv()
        if k == 1:
            s["x1m"].wait_recv()
        own = part[h, 2, 2 + k, r_x]
        xsm[h, k, w_a] = (f32(xb[h, 2, k, w_a]) + f32(own[:XH])).astype(BF16)
        xsm[h, k, w_b] = (f32(xb[h, 2, k, w_b]) + f32(own[XH:]) + f32(x1m[h, k])).astype(BF16)
        s["x2m", k] = send(xsm.at[h, k], x2m.at[h, k], down)

    def zsum(h, g):
        s, at = rs[h], pair[g]
        for name in ("plain_p", "plain_m", "sum_p", "sum_m"):
            s[name, g].wait_recv()
        return f32(part[h, 3, at, r_z]) + f32(z2p[h, at]) + f32(z2m[h, at])

    def z_given(h):
        xs[h] = zsum(h, 0).astype(BF16)
        for k in (1, 0):
            rs[h]["xs", k] = send(xs.at[h, k], xr.at[h, k], twin)
            rs[h]["xhop", 3, k] = send(part.at[h, 3, k, r_x], xb.at[h, 3, k], twin)

    def lanes(h):
        return pl.ds(h * WIDE, WIDE)

    def features(h):
        return pl.ds(pl.multiple_of(feat * 256 + h * WIDE, WIDE), WIDE)

    def z_done(h, k):
        s = rs[h]
        value = zsum(h, 2 - k)[0]
        s["xs", k].wait_recv()
        value = (value + f32(xr[h, k])).astype(BF16)
        if k == 1:
            give[r_z, lanes(h)] = value
            s["give_z"] = send(give.at[r_z, lanes(h)], hidden.at[r_z, features(h)], cross)
        else:
            hidden[r_z, features(h)] = value

    def x_done(h, k):
        s = rs[h]
        for name in (("xhop", 3, k), ("x2p", k), ("x2m", k)):
            s[name].wait_recv()
        value = (
            f32(xb[h, 3, k]) + f32(part[h, 3, 2 + k, r_x]) + f32(x2p[h, k]) + f32(x2m[h, k])
        ).astype(BF16)
        if k == 1:
            give[r_x, lanes(h)] = value
            s["give_x"] = send(give.at[r_x, lanes(h)], hidden.at[r_x, features(h)], cross)
        else:
            hidden[r_x, features(h)] = value

    def reduce_start(h):
        collect(h, 0, 1)
        xhop(h, 0)
        for g in range(3):
            hop(h, g)
        collect(h, 1, 4)
        xhop(h, 1)
        plain(h, 0)
        xhop(h, 2)

    def kept(h, k):
        plain(h, 2 - k)
        sums(h, 2 - k)

    def weight_1():
        return [send(gw.at[:, (col + j) % 8], ar1.at[j - 1], others_c[j - 1]) for j in range(1, 8)]

    def weight_2(copies):
        for c in copies:
            c.wait_recv()
        acc = f32(gw[:, col])
        for j in range(7):
            acc = acc + f32(ar1[j])
        for r in range(8):
            ar2s[r] = acc[:, r * 8 : r * 8 + 8, :]
        return [send(ar2s.at[(row + j) % 8], ar2.at[j - 1], others_r[j - 1]) for j in range(1, 8)]

    def weight_3(copies):
        for c in copies:
            c.wait_recv()
        done = ar2s[row]
        for j in range(7):
            done = done + ar2[j]
        ar3[col] = done.reshape(16, 256).astype(BF16)
        return [send(ar3.at[col], ar3.at[col], others_c[j]) for j in range(7)]

    def weight_4(copies):
        for c in copies:
            c.wait_recv()
        ar4[row] = ar3[...]
        return [send(ar3, ar4.at[row], others_r[j]) for j in range(7)]

    zero = jnp.zeros((TILE, WIDE), F32)
    gather_far(1)
    for c in swap:
        c.wait_recv()
    term(lambda: other[0], lambda: other[1], 1 - feat)
    wc = weight_1()
    run = products(0, 0, 2, zero)
    gather_near(1)
    products(0, 2, 4, run)
    gather_last(1)
    reduce_start(0)
    gather_end(1)
    run = products(1, 0, 2, zero)
    sums(0, 0)
    wc = weight_2(wc)
    run = products(1, 2, 4, run)
    x_first(0)
    kept(0, 1)
    kept(0, 0)
    run = products(1, 4, 6, run)
    wc = weight_3(wc)
    z_given(0)
    products(1, 6, 8, run)
    x_second(0, 1)
    x_second(0, 0)
    reduce_start(1)
    wc = weight_4(wc)
    z_done(0, 1)
    z_done(0, 0)
    x_done(0, 1)
    x_done(0, 0)
    sums(1, 0)
    x_first(1)
    kept(1, 1)
    z_given(1)
    x_second(1, 1)
    kept(1, 0)
    x_second(1, 0)
    z_done(1, 1)
    x_done(1, 1)
    z_done(1, 0)
    for c in wc:
        c.wait_recv()
    out = [pltpu.make_async_copy(ar4, pieces_hbm, lsem.at[0])]
    out[0].start()
    x_done(1, 0)
    for at, name in ((r_z, "give_z"), (r_x, "give_x")):
        for h in range(2):
            rs[h][name].wait_recv()
        out.append(pltpu.make_async_copy(hidden.at[at], hidden_hbm.at[at], lsem.at[len(out)]))
        out[-1].start()
    for c in out:
        c.wait()
    for c in started:
        c.wait_send()


def finish_kernel(
    hidden, weight, pieces, grad_in, grad_weight, hidden_v, weight_v, pieces_v, left, right, sems
):
    copies = [pltpu.make_async_copy(hidden, hidden_v, sems.at[0])]
    blocks = [pl.ds(n * 256, 256) for n in range(4)]
    for n, at in enumerate(blocks):
        copies.append(pltpu.make_async_copy(weight.at[at], weight_v.at[at], sems.at[1 + n]))
    copies.append(pltpu.make_async_copy(pieces, pieces_v, sems.at[5]))
    for i in (0, 1, 5, 2, 3, 4):
        copies[i].start()
    copies[0].wait()
    dims = (((1,), (1,)), ((), ()))
    out = []
    for n, at in enumerate(blocks):
        copies[1 + n].wait()
        left[:, at] = lax.dot_general(
            hidden_v[...], weight_v[at], dims, preferred_element_type=F32
        ).astype(BF16)
        out.append(pltpu.make_async_copy(left.at[:, at], grad_in.at[:, at], sems.at[6 + n]))
        out[-1].start()
        if n == 0:
            copies[5].wait()
            for s in range(8):
                for r in range(8):
                    piece = pieces_v[r, s].astype(F32)
                    rows = s * 64 + r * 8
                    for f in range(2):
                        right[rows : rows + 8, f * 256 : f * 256 + 256] = piece[f * 8 : f * 8 + 8]
            out.append(pltpu.make_async_copy(right, grad_weight, sems.at[10]))
            out[-1].start()
    for c in out:
        c.wait()


def finish(hidden, weight, pieces):
    anywhere = pl.BlockSpec(memory_space=pl.ANY)
    return pl.pallas_call(
        finish_kernel,
        in_specs=[anywhere] * 3,
        out_specs=(anywhere, anywhere),
        out_shape=(
            jax.ShapeDtypeStruct((512, 1024), BF16),
            jax.ShapeDtypeStruct((512, 512), F32),
        ),
        scratch_shapes=[
            pltpu.VMEM((512, 512), BF16),
            pltpu.VMEM((1024, 512), BF16),
            pltpu.VMEM((8, 8, 16, 256), BF16),
            pltpu.VMEM((512, 1024), BF16),
            pltpu.VMEM((512, 512), F32),
            pltpu.SemaphoreType.DMA((11,)),
        ],
        compiler_params=pltpu.CompilerParams(vmem_limit_bytes=60 * 2**20),
        name="finish",
    )(hidden, weight, pieces)


COPIES = 2 * 11 + 2 + 2 * 33 + 28


def per_device(grad_out, saved_agg, tile_values, tile_rows, tile_cols, tile_counts, weight):
    anywhere = pl.BlockSpec(memory_space=pl.ANY)
    scratch = [
        ((SLOTS + 1, TILE, TILE), BF16),
        ((64, TILE, WIDE), BF16), ((64, TILE, WIDE), BF16),
        ((STEPS + 1, TILE, WIDE), BF16), ((2, 4, 4, 512, WIDE), BF16),
        ((2, 4, ZH, WIDE), BF16), ((2, 4, ZH, WIDE), BF16),
        ((2, 4, ZR, WIDE), BF16), ((2, 4, ZR, WIDE), BF16),
        ((2, 4, ZH, WIDE), BF16), ((2, 4, ZH, WIDE), BF16),
        ((2, 2, ZR, WIDE), BF16), ((2, 2, ZR, WIDE), BF16),
        ((2, 4, 2, XR, WIDE), BF16),
        ((2, 2, XH, WIDE), BF16), ((2, 2, XH, WIDE), BF16),
        ((2, 2, XR, WIDE), BF16), ((2, 2, XR, WIDE), BF16),
        ((2, 2, XR, WIDE), BF16), ((2, 2, XR, WIDE), BF16), ((2, 2, XR, WIDE), BF16),
        ((512, 256), BF16), ((512, 512), BF16), ((8, TILE, 256), BF16), ((1024, 512), BF16), ((2, 8, TILE, WIDE), BF16),
        ((2, 8, 64, 256), BF16),
        ((7, 2, 64, 256), BF16), ((8, 2, 8, 256), F32), ((7, 2, 8, 256), F32),
        ((8, 16, 256), BF16), ((8, 8, 16, 256), BF16),
        ((1, SLOTS), I32), ((1, SLOTS), I32), ((1, 1), I32), ((1, PLACES), I32), ((1, TILE), I32),
    ]
    hidden, pieces = pl.pallas_call(
        fused_kernel,
        out_shape=(
            jax.ShapeDtypeStruct((512, 512), BF16),
            jax.ShapeDtypeStruct((8, 8, 16, 256), BF16),
        ),
        in_specs=[anywhere] * 6,
        out_specs=(anywhere, anywhere),
        scratch_shapes=[pltpu.VMEM(s, t) for s, t in scratch]
        + [pltpu.SMEM((1, PLACES), I32), pltpu.SMEM((1, TILE), I32)]
        + [
            pltpu.SemaphoreType.DMA((COPIES,)),
            pltpu.SemaphoreType.DMA((COPIES,)),
            pltpu.SemaphoreType.DMA((25,)),
        ],
        compiler_params=pltpu.CompilerParams(
            collective_id=0, has_side_effects=True, vmem_limit_bytes=56 * 2**20
        ),
        name="fused",
    )(
        tile_rows[0], tile_cols[0], tile_counts,
        grad_out.reshape(8, TILE, 256), saved_agg, tile_values[0, 0],
    )
    return finish(hidden, weight, pieces)


def solution(mesh):
    in_specs = (
        P(("row", "col"), "feat"),
        P(("row", "col"), "feat"),
        P("row", "col", None, None, None),
        P("row", "col", None),
        P("row", "col", None),
        P("row", "col"),
        P(),
    )
    out_specs = (P(("row", "col", "feat"), None), P("feat", None))
    return jax.shard_map(
        per_device, mesh=mesh, in_specs=in_specs, out_specs=out_specs, check_vma=False
    )
```
